128 devices in a mesh: blk: 64 (over y_hi, z, x, core), grp: 2 (over y_lo).
Axes of the slice: x: 4, y: 4 (y_hi: 2, y_lo: 2; y = y_hi * 2 + y_lo), z: 4, core: 2. Of those that a mesh axis runs over, the one named last changes fastest.
Arguments:
- points: float32 [3, 98304], P(None, 'blk'), may hold values from 0 to 8, as said below
- targets: float32 [16, 98304], P(None, 'blk'), may hold values from -64 to 64
- length_scales: float32 [3], replicated, may hold values from 1 to 2
- noise_levels: float32 [8], replicated, may hold values from 0.05 to 1
- noise_class: int32 [98304], P('blk'), may hold values from 0 to 7
Outputs:
- solution: float32 [16, 98304], P(None, 'blk')
- residual: float32 [16, 98304], P(None, 'blk')
The draws below stay inside these ranges and needn't reach their ends.
Inputs may be any that keep to these rules, and one draw needn't show every extreme that they name: `points`: each coordinate of each point lies in [0, 8].
All inputs are finite; a program needn't handle non-finite values.
Results may differ from the reference program's by a relative error of at most 0.00028.
Values sent between devices are 32-bit elements; how exact they have to be, the bound alone decides.
No kernel may reach another device: no remote copies, remote signals or barrier semaphores. Data moves between devices by JAX's collectives and lax.ppermute only.
A program may use at most 64 MiB of HBM per device.

```python
import math
import jax
import jax.numpy as jnp
from jax import lax

NVEC = 16
NCLS = 8
ITERS = 1
POINTS = 98304


def draw_points(key, part):
    key = jax.random.fold_in(key, 11)
    uniform_draw = jax.random.uniform(key, (3, POINTS), jnp.float32)
    return uniform_draw * 8.0


def draw_targets(key, part):
    key = jax.random.fold_in(key, 23)
    normal_key = jax.random.fold_in(key, 0)
    values = jnp.clip(jax.random.normal(normal_key, (NVEC, POINTS), jnp.float32), -5.0, 5.0)
    rising = 1.0 + 2.0 * lax.broadcasted_iota(jnp.float32, (1, POINTS), 1) / (POINTS - 1)
    return values * rising


def plant(result, stream_key, smallest, top_value):
    place = [jax.random.randint(jax.random.fold_in(stream_key, axis), (), 0, length) for axis, length in enumerate(result.shape)]
    longest = result.shape.index(max(result.shape))
    next_to = place[:longest] + [(place[longest] + 1) % result.shape[longest]] + place[longest + 1:]
    return result.at[tuple(place)].set(smallest).at[tuple(next_to)].set(top_value)


def setup_inputs(seed: int = 0) -> dict:
    arg_keys = jax.random.split(jax.random.key(seed), 6)
    return {
        "points": draw_points(jax.random.fold_in(arg_keys[5], 71), 0),
        "targets": draw_targets(jax.random.fold_in(arg_keys[5], 71), 0),
        "length_scales": jnp.clip(jax.random.uniform(arg_keys[2], (3,), jnp.float32, 1.0, 2.0), 1.0, 2.0),
        "noise_levels": jnp.clip(jnp.exp(jax.random.uniform(arg_keys[3], (NCLS,), jnp.float32, math.log(0.05), math.log(1.0))), 0.05, 1.0),
        "noise_class": plant(jax.random.randint(arg_keys[4], (POINTS,), 0, NCLS), jax.random.fold_in(arg_keys[4], 1), 0, NCLS - 1).astype(jnp.int32),
    }


def matern(row_points, col_points, inverse_scale):
    scaled_rows = row_points * inverse_scale[:, None]
    scaled_cols = col_points * inverse_scale[:, None]
    offsets = scaled_rows[0][:, None] - scaled_cols[0][None, :]
    squared = offsets * offsets
    offsets = scaled_rows[1][:, None] - scaled_cols[1][None, :]
    squared = squared + offsets * offsets
    offsets = scaled_rows[2][:, None] - scaled_cols[2][None, :]
    squared = squared + offsets * offsets
    radius = jnp.sqrt(5.0 * squared)
    return (1.0 + radius + radius * radius / 3.0) * jnp.exp(-radius)

def apply_kernel(points, vectors, noise_diag, inverse_scale):
    blocks = points.reshape(3, POINTS // 256, 256).transpose(1, 0, 2)

    def one_block(block_points):
        kernel_tile = matern(block_points, points, inverse_scale)
        return lax.dot_general(vectors, kernel_tile, (((1,), (1,)), ((), ())), precision=lax.Precision.HIGHEST, preferred_element_type=jnp.float32)
    stacked = lax.map(one_block, blocks)
    return stacked.transpose(1, 0, 2).reshape(vectors.shape) + noise_diag[None, :] * vectors

def reference(points, targets, length_scales, noise_levels, noise_class):
    inverse_scale = 1.0 / length_scales
    noise_diag = noise_levels[noise_class]
    solution = jnp.zeros_like(targets)
    residual = targets
    direction = targets
    norm_now = lax.optimization_barrier(jnp.sum(residual * residual, axis=1))
    for iteration in range(ITERS):
        kernel_image = apply_kernel(points, direction, noise_diag, inverse_scale)
        step_size = norm_now / lax.optimization_barrier(jnp.sum(direction * kernel_image, axis=1))
        solution = solution + step_size[:, None] * direction
        residual = residual - step_size[:, None] * kernel_image
        norm_next = lax.optimization_barrier(jnp.sum(residual * residual, axis=1))
        direction = residual + (norm_next / norm_now)[:, None] * direction
        norm_now = norm_next
    return (solution, residual)
```

```python
import math

import jax
import jax.numpy as jnp
import numpy as np
from jax import lax
from jax.experimental import pallas as pl
from jax.experimental.pallas import tpu as pltpu
from jax.sharding import PartitionSpec as P

BOTH = ("blk", "grp")
SHARD = 1536
CHUNKS = 4
SUPER = SHARD * CHUNKS
NSUPER = 16
NVEC = 16
TILE = 512
SUB = 256
LOG2E = math.log2(math.e)
SHIFT = 1.5 * LOG2E
OFFSET = 0.75 * LOG2E * LOG2E
FACTOR = 2.0**SHIFT / (3.0 * LOG2E * LOG2E)
bf16 = jnp.bfloat16
f32 = jnp.float32


def device_at(block, member):
    return (CHUNKS * block + member // 2) * 2 + member % 2


def column_route(chunk):
    route = []
    for a in range(NSUPER):
        for d in range(8):
            source = (a + (d if d else 8)) % NSUPER
            member = ((d // 2 + chunk) % CHUNKS) * 2 + d % 2
            route.append((device_at(source, member), device_at(a, d)))
    return route


def row_route(chunk):
    return [
        (device_at(a, ((d // 2 + chunk) % CHUNKS) * 2 + d % 2), device_at(a, d))
        for a in range(NSUPER)
        for d in range(8)
    ]


def backward(route):
    return [(b, a) for a, b in route]


def tile_tables():
    per = SHARD // TILE
    side = SUPER // TILE
    triangle = [(i, j) for i in range(side) for j in range(i, side)]
    cuts = [0, 20, 40, 60, 78]
    tables, counts = [], []
    for call in range(CHUNKS):
        first = SUPER // TILE
        regular = [(i, first + j, 1) for i in range(side) for j in range(per)]
        lists = [regular]
        for distances in ((0, 1), (1, 2)):
            tiles = []
            for distance in distances:
                chunk = (call - distance) % CHUNKS
                tiles += [(chunk * per + i, first + j, 1) for i in range(per) for j in range(per)]
            tiles += [(i, j, int(i != j)) for i, j in triangle[cuts[call] : cuts[call + 1]]]
            lists.append(tiles)
        longest = max(len(x) for x in lists)
        counts.append([len(x) for x in lists])
        assert all(len(x) % 2 == 0 for x in lists)
        tables.append(
            np.array(
                [[(i * TILE, j * TILE, k) for i, j, k in x + x[:1] * (longest - len(x))] for x in lists],
                np.int32,
            )
        )
    return tables, counts


def pieces(value, count):
    out = []
    for _ in range(count):
        piece = value.astype(bf16).astype(f32)
        out.append(piece)
        value = value - piece
    return out


def kernel_values(squared):
    squared = jnp.maximum(squared, 1e-12)
    shifted = -SHIFT - squared * lax.rsqrt(squared)
    return (shifted * shifted + OFFSET) * jnp.exp2(shifted)


def tile_kernel(
    table, meta, scale, x0, x1, x2, x3, y0, sums_in, curve_in,
    sums_out, column_out, curve_out,
    row_feat, col_feat, col_vec, row_vec_t, row_sum, col_sum, hi0, hi1, lo0, lo1,
):
    chunks = [x0, x1, x2, x3, y0]
    for place, chunk in enumerate(chunks):
        span = slice(place * SHARD, (place + 1) * SHARD)
        scaled = jnp.concatenate(
            [(chunk[c : c + 1, :] - 4.0) * scale[c] for c in range(3)], axis=0
        )
        a1, a2, a3 = pieces(scaled, 3)
        norm = jnp.sum(scaled * scaled, axis=0, keepdims=True)
        n1, n2, n3 = pieces(norm, 3)
        one = jnp.ones_like(norm)
        pad = jnp.zeros((8, SHARD), f32)
        columns = jnp.concatenate(
            [-2.0 * a1, -2.0 * a2, -2.0 * a1, -2.0 * a3, -2.0 * a2, -2.0 * a1,
             one, one, one, n1, n2, n3, pad], axis=0)
        col_feat[:, span] = columns.astype(bf16)
        vec_hi, vec_lo = pieces(chunk[3:19, :], 2)
        vec = jnp.concatenate([vec_hi, vec_lo], axis=0)
        col_vec[span, :] = jnp.transpose(vec).astype(bf16)
        if place < CHUNKS:
            rows = jnp.concatenate(
                [a1, a1, a2, a1, a2, a3, n1, n2, n3, one, one, one, pad], axis=0
            )
            row_feat[span, :] = jnp.transpose(rows).astype(bf16)
            row_vec_t[:, span] = vec.astype(bf16)
    for ref in (row_sum, col_sum, hi0, hi1, lo0, lo1):
        ref[...] = jnp.zeros_like(ref)
    variant = meta[0]
    count = meta[1]

    def place_of(t):
        return (
            pl.multiple_of(table[variant, t, 0], TILE),
            pl.multiple_of(table[variant, t, 1], TILE),
            table[variant, t, 2],
        )

    def produce(place, hi, lo, x):
        row, col, _ = place
        right = col_feat[:, pl.ds(pl.multiple_of(col + x, SUB), SUB)]
        for y in range(0, TILE, SUB):
            left = row_feat[pl.ds(pl.multiple_of(row + y, SUB), SUB), :]
            value = kernel_values(jnp.dot(left, right, preferred_element_type=f32))
            high = value.astype(bf16)
            hi[y : y + SUB, x : x + SUB] = high
            lo[y : y + SUB, x : x + SUB] = (value - high.astype(f32)).astype(bf16)

    def consume(place, hi, lo, x, total):
        row, col, keep = place
        span = pl.ds(pl.multiple_of(col + x, SUB), SUB)
        high, low = hi[:, x : x + SUB], lo[:, x : x + SUB]
        right = col_vec[span, :]
        part = jnp.dot(high, right, preferred_element_type=f32)
        part = part + jnp.dot(low, right, preferred_element_type=f32)
        left = row_vec_t[:, pl.ds(row, TILE)]
        column = jnp.dot(left, high, preferred_element_type=f32)
        column = column + jnp.dot(left, low, preferred_element_type=f32)
        col_sum[:, span] += column * keep.astype(f32)
        return part if total is None else total + part

    def both(ahead, ahead_hi, ahead_lo, now, hi, lo):
        total = None
        for x in range(0, TILE, SUB):
            if ahead is not None:
                produce(ahead, ahead_hi, ahead_lo, x)
            total = consume(now, hi, lo, x, total)
        row_sum[pl.ds(now[0], TILE), :] += total

    def two_tiles(u, carried):
        both(place_of(2 * u), hi0, lo0, place_of(jnp.maximum(2 * u - 1, 0)), hi1, lo1)
        both(place_of(2 * u + 1), hi1, lo1, place_of(2 * u), hi0, lo0)
        return carried

    lax.fori_loop(0, count // 2, two_tiles, 0)
    both(None, None, None, place_of(count - 1), hi1, lo1)

    curve = curve_in[...]
    for place, chunk in enumerate(chunks):
        span = slice(place * SHARD, (place + 1) * SHARD)
        total = col_sum[:, span]
        if place < CHUNKS:
            total = total + jnp.transpose(row_sum[span, :])
        total = FACTOR * (total[:NVEC] + total[NVEC:])
        product = total * chunk[3:19, :]
        for lane in range(0, SHARD, 128):
            curve = curve + product[:, lane : lane + 128]
        if place < CHUNKS:
            sums_out[:, span] = sums_in[:, span] + total
        else:
            column_out[...] = total
    curve_out[...] = curve


def run_tiles(table, meta, scale, rows, columns, sums, curve):
    vmem = pl.BlockSpec(memory_space=pltpu.VMEM)
    smem = pl.BlockSpec(memory_space=pltpu.SMEM)
    every = SUPER + SHARD
    return pl.pallas_call(
        tile_kernel,
        out_shape=[
            jax.ShapeDtypeStruct((NVEC, SUPER), f32),
            jax.ShapeDtypeStruct((NVEC, SHARD), f32),
            jax.ShapeDtypeStruct((NVEC, 128), f32),
        ],
        in_specs=[smem] * 3 + [vmem] * 7,
        out_specs=[vmem] * 3,
        scratch_shapes=[
            pltpu.VMEM((SUPER, 32), bf16),
            pltpu.VMEM((32, every), bf16),
            pltpu.VMEM((every, 32), bf16),
            pltpu.VMEM((32, SUPER), bf16),
            pltpu.VMEM((SUPER, 32), f32),
            pltpu.VMEM((32, every), f32),
        ]
        + [pltpu.VMEM((TILE, TILE), bf16)] * 4,
        compiler_params=pltpu.CompilerParams(vmem_limit_bytes=56 * 2**20),
        cost_estimate=pl.CostEstimate(
            flops=30_000_000_000, bytes_accessed=2_000_000, transcendentals=0
        ),
    )(table, meta, scale, *rows, columns, sums, curve)


def on_device(points, targets, length_scales, noise_levels, noise_class):
    shard = jnp.concatenate([points, targets], axis=0)
    columns = [lax.ppermute(shard, BOTH, column_route(c)) for c in range(CHUNKS)]
    rows = [shard] + [lax.ppermute(shard, BOTH, row_route(c)) for c in range(1, CHUNKS)]

    block = lax.axis_index("blk")
    first = (block % CHUNKS == 0) & (lax.axis_index("grp") == 0)
    variant = jnp.where(first, jnp.where(block < 32, 1, 2), 0).astype(jnp.int32)
    tables, counts = tile_tables()
    scale = (math.sqrt(5.0) * LOG2E) / length_scales

    sums = jnp.zeros((NVEC, SUPER), f32)
    curve = jnp.zeros((NVEC, 128), f32)
    returned = []
    for c in range(CHUNKS):
        count = jnp.where(variant == 0, counts[c][0], counts[c][1]).astype(jnp.int32)
        meta = jnp.stack([variant, count])
        sums, column_sums, curve = run_tiles(
            jnp.asarray(tables[c]), meta, scale, rows, columns[c], sums, curve
        )
        returned.append(lax.ppermute(column_sums, BOTH, backward(column_route(c))))
    for c in range(1, CHUNKS):
        part = sums[:, c * SHARD : (c + 1) * SHARD]
        returned.append(lax.ppermute(part, BOTH, backward(row_route(c))))

    classes = lax.broadcasted_iota(jnp.int32, (noise_levels.shape[0], noise_class.shape[0]), 0)
    noise_diag = jnp.sum(
        jnp.where(noise_class[None, :] == classes, noise_levels[:, None], 0.0), axis=0
    )
    own_noise = noise_diag[None, :] * targets
    norm = 0.5 * jnp.sum(targets * targets, axis=1)
    curvature = jnp.sum(curve, axis=1) + 0.5 * jnp.sum(targets * own_noise, axis=1)
    scalars = jnp.stack([norm, curvature])
    for k in range(6):
        scalars = scalars + lax.ppermute(scalars, "blk", [(i, i ^ (1 << k)) for i in range(64)])
    scalars = scalars + lax.ppermute(scalars, "grp", [(0, 1), (1, 0)])
    step_size = scalars[0] / scalars[1]

    own = sums[:, :SHARD]
    for part in returned:
        own = own + part
    image = own + lax.ppermute(own, "grp", [(0, 1), (1, 0)]) + own_noise
    return (step_size[:, None] * targets, targets - step_size[:, None] * image)


def solution(mesh):
    return jax.shard_map(
        on_device,
        mesh=mesh,
        in_specs=(P(None, "blk"), P(None, "blk"), P(), P(), P("blk")),
        out_specs=(P(None, "blk"), P(None, "blk")),
        check_vma=False,
    )
```

```python
import functools
import math

import jax
import jax.numpy as jnp
import numpy as np
from jax import lax
from jax.experimental import pallas as pl
from jax.experimental.pallas import tpu as pltpu
from jax.sharding import PartitionSpec as P

BOTH = ("blk", "grp")
SHARD = 1536
CHUNKS = 4
SUPER = SHARD * CHUNKS
NSUPER = 16
NVEC = 16
TILE = 512
SUB = 256
LOG2E = math.log2(math.e)
SHIFT = 1.5 * LOG2E
OFFSET = 0.75 * LOG2E * LOG2E
FACTOR = 2.0**SHIFT / (3.0 * LOG2E * LOG2E)
bf16 = jnp.bfloat16
f32 = jnp.float32


def device_at(block, member):
    return (CHUNKS * block + member // 2) * 2 + member % 2


def column_route(chunk):
    route = []
    for a in range(NSUPER):
        for d in range(8):
            source = (a + (d if d else 8)) % NSUPER
            member = ((d // 2 + chunk) % CHUNKS) * 2 + d % 2
            route.append((device_at(source, member), device_at(a, d)))
    return route


def row_route(chunk):
    return [
        (device_at(a, ((d // 2 + chunk) % CHUNKS) * 2 + d % 2), device_at(a, d))
        for a in range(NSUPER)
        for d in range(8)
    ]


def backward(route):
    return [(b, a) for a, b in route]


CALLS = [((0, 1, 2, 3), (0,)), ((0, 1, 2, 3), (1,)), ((1, 2, 3), (2, 3)), ((0,), (2, 3))]
OFF = [(1, 0), (2, 1), (3, 1), (0, 2), (0, 3), (2, 3)]
ON = [[(0, 0), (1, 1)], [(2, 2), (3, 3)]]
FILL = [[20, 11, 47, 0], [29, 20, 29, 0]]


def tile_tables():
    per = SHARD // TILE
    side = SUPER // TILE
    triangle = [(i, j) for i in range(side) for j in range(i, side)]
    used = [0, 0]
    tables, counts = [], []
    for call, (rows, columns) in enumerate(CALLS):
        held = (0, 1, 2, 3) if len(rows) > 1 else rows

        def pair(i, j):
            first = (len(held) + columns.index(j)) * per
            return [
                (held.index(i) * per + y, first + x, 1) for y in range(per) for x in range(per)
            ]

        lists = [[t for i in rows for j in columns for t in pair(i, j)]]
        for half in range(2):
            chunks = [(i, j) for i, j in OFF + ON[half] if i in rows and j in columns]
            tiles = [t for i, j in chunks for t in pair(i, j)]
            part = triangle[used[half] : used[half] + FILL[half][call]]
            used[half] += len(part)
            tiles += [(i, j, int(i != j)) for i, j in part]
            lists.append(tiles)
        longest = max(len(x) for x in lists)
        counts.append([len(x) for x in lists])
        assert all(len(x) % 2 == 0 for x in lists)
        tables.append(
            np.array(
                [
                    [(i * TILE, j * TILE, k) for i, j, k in x + x[:1] * (longest - len(x))]
                    for x in lists
                ],
                np.int32,
            )
        )
    assert used == [len(triangle)] * 2
    return tables, counts


def pieces(value, count):
    out = []
    for _ in range(count):
        piece = value.astype(bf16).astype(f32)
        out.append(piece)
        value = value - piece
    return out


def kernel_values(squared):
    squared = jnp.maximum(squared, 1e-12)
    shifted = -SHIFT - squared * lax.rsqrt(squared)
    return (shifted * shifted + OFFSET) * jnp.exp2(shifted)


def tile_kernel(x_count, y_count, chained, *refs):
    refs = list(refs)
    table, meta, scale = refs[:3]
    chunks = refs[3 : 3 + x_count + y_count]
    rest = refs[3 + x_count + y_count :]
    if chained:
        sums_in, curve_in, rest = rest[:x_count], rest[x_count], rest[x_count + 1 :]
    sums_out, rest = rest[: x_count + y_count], rest[x_count + y_count :]
    curve_out, row_feat, col_feat, vectors, row_sum, col_sum, hi0, hi1, lo0, lo1 = rest

    for place, chunk in enumerate(chunks):
        span = slice(place * SHARD, (place + 1) * SHARD)
        scaled = jnp.concatenate(
            [(chunk[c : c + 1, :] - 4.0) * scale[c] for c in range(3)], axis=0
        )
        a1, a2, a3 = pieces(scaled, 3)
        norm = jnp.sum(scaled * scaled, axis=0, keepdims=True)
        n1, n2, n3 = pieces(norm, 3)
        one = jnp.ones_like(norm)
        pad = jnp.zeros((8, SHARD), f32)
        columns = jnp.concatenate(
            [-2.0 * a1, -2.0 * a2, -2.0 * a1, -2.0 * a3, -2.0 * a2, -2.0 * a1,
             one, one, one, n1, n2, n3, pad], axis=0)
        col_feat[:, span] = columns.astype(bf16)
        vectors[:, span] = jnp.concatenate(pieces(chunk[3:19, :], 2), axis=0).astype(bf16)
        if place < x_count:
            rows = jnp.concatenate(
                [a1, a1, a2, a1, a2, a3, n1, n2, n3, one, one, one, pad], axis=0
            )
            row_feat[span, :] = jnp.transpose(rows).astype(bf16)
    for ref in (row_sum, col_sum, hi1, lo1):
        ref[...] = jnp.zeros_like(ref)
    variant = meta[0]
    count = meta[1]

    def place_of(t):
        return (
            pl.multiple_of(table[variant, t, 0], TILE),
            pl.multiple_of(table[variant, t, 1], TILE),
            table[variant, t, 2],
        )

    def produce(place, hi, lo, x):
        row, col, _ = place
        right = col_feat[:, pl.ds(pl.multiple_of(col + x, SUB), SUB)]
        for y in range(0, TILE, SUB):
            left = row_feat[pl.ds(pl.multiple_of(row + y, SUB), SUB), :]
            value = kernel_values(jnp.dot(left, right, preferred_element_type=f32))
            high = value.astype(bf16)
            hi[y : y + SUB, x : x + SUB] = high
            lo[y : y + SUB, x : x + SUB] = (value - high.astype(f32)).astype(bf16)

    def consume(place, hi, lo, x):
        row, col, keep = place
        across = (((1,), (1,)), ((), ()))
        span = pl.ds(pl.multiple_of(col + x, SUB), SUB)
        high, low = hi[:, x : x + SUB], lo[:, x : x + SUB]
        far, near = vectors[:, span], vectors[:, pl.ds(row, TILE)]
        part = lax.dot_general(far, high, across, preferred_element_type=f32)
        part = part + lax.dot_general(far, low, across, preferred_element_type=f32)
        row_sum[:, pl.ds(row, TILE)] += part
        part = jnp.dot(near, high, preferred_element_type=f32)
        part = part + jnp.dot(near, low, preferred_element_type=f32)
        col_sum[:, span] += part * keep.astype(f32)

    def both(ahead, ahead_hi, ahead_lo, now, hi, lo):
        for x in range(0, TILE, SUB):
            if ahead is not None:
                produce(ahead, ahead_hi, ahead_lo, x)
            consume(now, hi, lo, x)

    def two_tiles(u, carried):
        both(place_of(2 * u), hi0, lo0, place_of(jnp.maximum(2 * u - 1, 0)), hi1, lo1)
        both(place_of(2 * u + 1), hi1, lo1, place_of(2 * u), hi0, lo0)
        return carried

    lax.fori_loop(0, count // 2, two_tiles, 0)
    both(None, None, None, place_of(count - 1), hi1, lo1)

    curve = curve_in[...] if chained else jnp.zeros((NVEC, 128), f32)
    for place, chunk in enumerate(chunks):
        span = slice(place * SHARD, (place + 1) * SHARD)
        total = col_sum[:, span]
        if place < x_count:
            total = total + row_sum[:, span]
        total = FACTOR * (total[:NVEC] + total[NVEC:])
        product = total * chunk[3:19, :]
        for lane in range(0, SHARD, 128):
            curve = curve + product[:, lane : lane + 128]
        if chained and place < x_count:
            total = total + sums_in[place][...]
        sums_out[place][...] = total
    curve_out[...] = curve


def run_tiles(table, meta, scale, rows, columns, sums, curve):
    vmem = pl.BlockSpec(memory_space=pltpu.VMEM)
    smem = pl.BlockSpec(memory_space=pltpu.SMEM)
    count = len(rows) + len(columns)
    wide = len(rows) * SHARD
    every = count * SHARD
    chained = curve is not None
    passed = [*rows, *columns, *sums, curve] if chained else [*rows, *columns]
    out = pl.pallas_call(
        functools.partial(tile_kernel, len(rows), len(columns), chained),
        out_shape=[jax.ShapeDtypeStruct((NVEC, SHARD), f32)] * count
        + [jax.ShapeDtypeStruct((NVEC, 128), f32)],
        in_specs=[smem] * 3 + [vmem] * len(passed),
        out_specs=[vmem] * (count + 1),
        scratch_shapes=[
            pltpu.VMEM((wide, 32), bf16),
            pltpu.VMEM((32, every), bf16),
            pltpu.VMEM((32, every), bf16),
            pltpu.VMEM((32, wide), f32),
            pltpu.VMEM((32, every), f32),
        ]
        + [pltpu.VMEM((TILE, TILE), bf16)] * 4,
        compiler_params=pltpu.CompilerParams(vmem_limit_bytes=48 * 2**20),
        cost_estimate=pl.CostEstimate(
            flops=800_000_000 * table.shape[1], bytes_accessed=2_000_000, transcendentals=0
        ),
    )(table, meta, scale, *passed)
    return out[: len(rows)], out[len(rows) : count], out[count]


def summed_over_devices(value, own):
    def along(value, axis, size, masks):
        routes = [[(i, i ^ mask) for i in range(size)] for mask in masks]
        parts = [lax.ppermute(value, axis, route) for route in routes]
        return value, parts

    def added(value, parts):
        if len(parts) == 1:
            return value + parts[0]
        return (value + parts[0]) + (parts[1] + parts[2])

    value = added(*along(value, "blk", 64, [1]))
    value = added(*along(value, "blk", 64, [2, 4, 6]))
    value, own = lax.optimization_barrier((value, own))
    value = added(*along(value, "blk", 64, [8, 16, 24]))
    value = added(*along(value, BOTH, 128, [1, 64, 65]))
    return value, own


def on_device(points, targets, length_scales, noise_levels, noise_class):
    shard = jnp.concatenate([points, targets], axis=0)
    columns = [lax.ppermute(shard, BOTH, column_route(c)) for c in range(CHUNKS)]
    rows = [shard] + [lax.ppermute(shard, BOTH, row_route(c)) for c in range(1, CHUNKS)]

    block = lax.axis_index("blk")
    first = (block % CHUNKS == 0) & (lax.axis_index("grp") == 0)
    variant = jnp.where(first, jnp.where(block < 32, 1, 2), 0).astype(jnp.int32)
    tables, counts = tile_tables()
    scale = (math.sqrt(5.0) * LOG2E) / length_scales

    sums, curve = None, None
    column_sums = {}
    returned = []
    for call, (row_chunks, column_chunks) in enumerate(CALLS):
        count = jnp.where(variant == 0, counts[call][0], counts[call][1]).astype(jnp.int32)
        meta = jnp.stack([variant, count])
        held = rows if len(row_chunks) > 1 else [rows[c] for c in row_chunks]
        before = sums if len(row_chunks) > 1 else [sums[c] for c in row_chunks]
        after, column_part, curve = run_tiles(
            jnp.asarray(tables[call]), meta, scale, held, [columns[c] for c in column_chunks],
            before, curve,
        )
        if len(row_chunks) > 1:
            sums = after
        for c, part in zip(column_chunks, column_part):
            column_sums[c] = column_sums[c] + part if c in column_sums else part
        if call == 2:
            for c in range(1, CHUNKS):
                returned.append(lax.ppermute(sums[c], BOTH, backward(row_route(c))))
        if call < 2:
            c = column_chunks[0]
            returned.append(lax.ppermute(column_sums[c], BOTH, backward(column_route(c))))
    last = [lax.ppermute(column_sums[c], BOTH, backward(column_route(c))) for c in (2, 3)]

    classes = lax.broadcasted_iota(jnp.int32, (noise_levels.shape[0], noise_class.shape[0]), 0)
    noise_diag = jnp.sum(
        jnp.where(noise_class[None, :] == classes, noise_levels[:, None], 0.0), axis=0
    )
    own_noise = noise_diag[None, :] * targets
    norm = 0.5 * jnp.sum(targets * targets, axis=1)
    curvature = jnp.sum(curve, axis=1) + 0.5 * jnp.sum(targets * own_noise, axis=1)

    own = after[0]
    for part in returned + last:
        own = own + part
    scalars, own = summed_over_devices(jnp.stack([norm, curvature]), own)
    step_size = scalars[0] / scalars[1]
    image = own + lax.ppermute(own, "grp", [(0, 1), (1, 0)]) + own_noise
    return (step_size[:, None] * targets, targets - step_size[:, None] * image)


def solution(mesh):
    return jax.shard_map(
        on_device,
        mesh=mesh,
        in_specs=(P(None, "blk"), P(None, "blk"), P(), P(), P("blk")),
        out_specs=(P(None, "blk"), P(None, "blk")),
        check_vma=False,
    )
```

```python
import functools
import math

import jax
import jax.numpy as jnp
import numpy as np
from jax import lax
from jax.experimental import pallas as pl
from jax.experimental.pallas import tpu as pltpu
from jax.sharding import PartitionSpec as P

BOTH = ("blk", "grp")
SHARD = 1536
CHUNKS = 4
SUPER = SHARD * CHUNKS
NSUPER = 16
NVEC = 16
TILE = 512
SUB = 256
LOG2E = math.log2(math.e)
SHIFT = 1.5 * LOG2E
OFFSET = 0.75 * LOG2E * LOG2E
FACTOR = 2.0**SHIFT / (3.0 * LOG2E * LOG2E)
bf16 = jnp.bfloat16
f32 = jnp.float32


def device_at(block, member):
    return (CHUNKS * block + member // 2) * 2 + member % 2


def column_route(chunk):
    route = []
    for a in range(NSUPER):
        for d in range(8):
            source = (a + (d if d else 8)) % NSUPER
            member = ((d // 2) ^ chunk) * 2 + d % 2
            route.append((device_at(source, member), device_at(a, d)))
    return route


def row_route(chunk):
    return [
        (device_at(a, ((d // 2) ^ chunk) * 2 + d % 2), device_at(a, d))
        for a in range(NSUPER)
        for d in range(8)
    ]


def backward(route):
    return [(b, a) for a, b in route]


CALLS = [
    ((0, 1), (0,), [(0, 0), (1, 0)]),
    ((0, 1, 2, 3), (0, 1), [(2, 0), (3, 0), (0, 1), (1, 1), (2, 1), (3, 1)]),
    ((0, 1, 2, 3), (2, 3), [(i, j) for i in (1, 2, 3) for j in (2, 3)]),
    ((0,), (2, 3), [(0, 2), (0, 3)]),
]
OFF = [(1, 0), (2, 1), (3, 1), (0, 2), (0, 3), (2, 3)]
ON = [[(0, 0), (1, 1)], [(2, 2), (3, 3)]]
FILL = [[0, 31, 47, 0], [9, 40, 29, 0]]


def tile_tables():
    per = SHARD // TILE
    side = SUPER // TILE
    triangle = [(i, j) for j in range(side) for i in range(j + 1)]
    used = [0, 0]
    tables, counts = [], []
    for call, (held, columns, pairs) in enumerate(CALLS):

        def pair(i, j):
            first = (len(held) + columns.index(j)) * per
            return [
                (held.index(i) * per + y, first + x, 1) for y in range(per) for x in range(per)
            ]

        lists = [[t for i, j in pairs for t in pair(i, j)]]
        for half in range(2):
            tiles = [t for i, j in OFF + ON[half] if (i, j) in pairs for t in pair(i, j)]
            part = triangle[used[half] : used[half] + FILL[half][call]]
            assert not part or max(j for _, j in part) < len(held) * per
            used[half] += len(part)
            tiles += [(i, j, int(i != j)) for i, j in part]
            lists.append(tiles)
        longest = max(len(x) for x in lists)
        counts.append([len(x) for x in lists])
        assert all(len(x) % 2 == 0 for x in lists) and counts[-1][1] == counts[-1][2]
        tables.append(
            np.array(
                [
                    [(i * TILE, j * TILE, k) for i, j, k in x + x[:1] * (longest - len(x))]
                    for x in lists
                ],
                np.int32,
            )
        )
    assert used == [len(triangle)] * 2
    return tables, counts


def pieces(value, count):
    out = []
    for _ in range(count):
        piece = value.astype(bf16).astype(f32)
        out.append(piece)
        value = value - piece
    return out


def kernel_values(squared):
    squared = jnp.maximum(squared, 1e-12)
    shifted = -SHIFT - squared * lax.rsqrt(squared)
    return (shifted * shifted + OFFSET) * jnp.exp2(shifted)


def tile_kernel(x_count, every, begun, *refs):
    refs = list(refs)
    table, meta, scale = refs[:3]
    chunks, rest = refs[3 : 3 + every], refs[3 + every :]
    sums_in, rest = dict(zip(begun, rest)), rest[len(begun) :]
    if begun:
        curve_in, rest = rest[0], rest[1:]
    sums_out, rest = rest[:every], rest[every:]
    curve_out, row_feat, col_feat, vectors, row_sum, col_sum, hi0, hi1, lo0, lo1 = rest

    for place, chunk in enumerate(chunks):
        span = slice(place * SHARD, (place + 1) * SHARD)
        scaled = jnp.concatenate(
            [(chunk[c : c + 1, :] - 4.0) * scale[c] for c in range(3)], axis=0
        )
        a1, a2, a3 = pieces(scaled, 3)
        norm = jnp.sum(scaled * scaled, axis=0, keepdims=True)
        n1, n2, n3 = pieces(norm, 3)
        one = jnp.ones_like(norm)
        pad = jnp.zeros((8, SHARD), f32)
        columns = jnp.concatenate(
            [-2.0 * a1, -2.0 * a2, -2.0 * a1, -2.0 * a3, -2.0 * a2, -2.0 * a1,
             one, one, one, n1, n2, n3, pad], axis=0)
        col_feat[:, span] = columns.astype(bf16)
        vectors[:, span] = jnp.concatenate(pieces(chunk[3:19, :], 2), axis=0).astype(bf16)
        if place < x_count:
            rows = jnp.concatenate(
                [a1, a1, a2, a1, a2, a3, n1, n2, n3, one, one, one, pad], axis=0
            )
            row_feat[span, :] = jnp.transpose(rows).astype(bf16)
    for ref in (row_sum, col_sum, hi1, lo1):
        ref[...] = jnp.zeros_like(ref)
    variant = meta[0]
    count = meta[1]

    def place_of(t):
        return (
            pl.multiple_of(table[variant, t, 0], TILE),
            pl.multiple_of(table[variant, t, 1], TILE),
            table[variant, t, 2],
        )

    def produce(place, hi, lo, x):
        row, col, _ = place
        right = col_feat[:, pl.ds(pl.multiple_of(col + x, SUB), SUB)]
        for y in range(0, TILE, SUB):
            left = row_feat[pl.ds(pl.multiple_of(row + y, SUB), SUB), :]
            value = kernel_values(jnp.dot(left, right, preferred_element_type=f32))
            high = value.astype(bf16)
            hi[y : y + SUB, x : x + SUB] = high
            lo[y : y + SUB, x : x + SUB] = (value - high.astype(f32)).astype(bf16)

    def consume(place, hi, lo, x):
        row, col, keep = place
        across = (((1,), (1,)), ((), ()))
        span = pl.ds(pl.multiple_of(col + x, SUB), SUB)
        high, low = hi[:, x : x + SUB], lo[:, x : x + SUB]
        far, near = vectors[:, span], vectors[:, pl.ds(row, TILE)]
        part = lax.dot_general(far, high, across, preferred_element_type=f32)
        part = part + lax.dot_general(far, low, across, preferred_element_type=f32)
        row_sum[:, pl.ds(row, TILE)] += part
        part = jnp.dot(near, high, preferred_element_type=f32)
        part = part + jnp.dot(near, low, preferred_element_type=f32)
        col_sum[:, span] += part * keep.astype(f32)

    def both(ahead, ahead_hi, ahead_lo, now, hi, lo):
        for x in range(0, TILE, SUB):
            if ahead is not None:
                produce(ahead, ahead_hi, ahead_lo, x)
            consume(now, hi, lo, x)

    def two_tiles(u, carried):
        both(place_of(2 * u), hi0, lo0, place_of(jnp.maximum(2 * u - 1, 0)), hi1, lo1)
        both(place_of(2 * u + 1), hi1, lo1, place_of(2 * u), hi0, lo0)
        return carried

    lax.fori_loop(0, count // 2, two_tiles, 0)
    both(None, None, None, place_of(count - 1), hi1, lo1)

    curve = curve_in[...] if begun else jnp.zeros((NVEC, 128), f32)
    for place, chunk in enumerate(chunks):
        span = slice(place * SHARD, (place + 1) * SHARD)
        total = col_sum[:, span]
        if place < x_count:
            total = total + row_sum[:, span]
        total = FACTOR * (total[:NVEC] + total[NVEC:])
        product = total * chunk[3:19, :]
        for lane in range(0, SHARD, 128):
            curve = curve + product[:, lane : lane + 128]
        if place in sums_in:
            total = total + sums_in[place][...]
        sums_out[place][...] = total
    curve_out[...] = curve


def run_tiles(table, meta, scale, rows, columns, sums, curve):
    vmem = pl.BlockSpec(memory_space=pltpu.VMEM)
    smem = pl.BlockSpec(memory_space=pltpu.SMEM)
    count = len(rows) + len(columns)
    wide = len(rows) * SHARD
    every = count * SHARD
    begun = tuple(i for i, part in enumerate(sums) if part is not None)
    passed = [*rows, *columns, *(sums[i] for i in begun)]
    if begun:
        passed.append(curve)
    out = pl.pallas_call(
        functools.partial(tile_kernel, len(rows), count, begun),
        out_shape=[jax.ShapeDtypeStruct((NVEC, SHARD), f32)] * count
        + [jax.ShapeDtypeStruct((NVEC, 128), f32)],
        in_specs=[smem] * 3 + [vmem] * len(passed),
        out_specs=[vmem] * (count + 1),
        scratch_shapes=[
            pltpu.VMEM((wide, 32), bf16),
            pltpu.VMEM((32, every), bf16),
            pltpu.VMEM((32, every), bf16),
            pltpu.VMEM((32, wide), f32),
            pltpu.VMEM((32, every), f32),
        ]
        + [pltpu.VMEM((TILE, TILE), bf16)] * 4,
        compiler_params=pltpu.CompilerParams(vmem_limit_bytes=48 * 2**20),
        cost_estimate=pl.CostEstimate(
            flops=800_000_000 * table.shape[1], bytes_accessed=2_000_000, transcendentals=0
        ),
    )(table, meta, scale, *passed)
    return out[:count], out[count]


def summed_over_devices(value, own):
    def along(value, axis, size, masks):
        routes = [[(i, i ^ mask) for i in range(size)] for mask in masks]
        parts = [lax.ppermute(value, axis, route) for route in routes]
        return value, parts

    def added(value, parts):
        if len(parts) == 1:
            return value + parts[0]
        return (value + parts[0]) + (parts[1] + parts[2])

    value = added(*along(value, "blk", 64, [1]))
    value = added(*along(value, "blk", 64, [2, 4, 6]))
    value, own = lax.optimization_barrier((value, own))
    value = added(*along(value, "blk", 64, [8, 16, 24]))
    value = added(*along(value, BOTH, 128, [1, 64, 65]))
    return value, own


def after(value, *others):
    return lax.optimization_barrier((value, *others))[0]


def on_device(points, targets, length_scales, noise_levels, noise_class):
    shard = jnp.concatenate([points, targets], axis=0)
    rows, columns = {0: shard}, {}
    columns[0] = lax.ppermute(shard, BOTH, column_route(0))
    rows[1] = lax.ppermute(shard, BOTH, row_route(1))
    then = after(shard, columns[0], rows[1])
    rows[2] = lax.ppermute(then, BOTH, row_route(2))
    rows[3] = lax.ppermute(then, BOTH, row_route(3))
    columns[1] = lax.ppermute(then, BOTH, column_route(1))

    block = lax.axis_index("blk")
    first = (block % CHUNKS == 0) & (lax.axis_index("grp") == 0)
    variant = jnp.where(first, jnp.where(block < 32, 1, 2), 0).astype(jnp.int32)
    tables, counts = tile_tables()
    scale = (math.sqrt(5.0) * LOG2E) / length_scales

    sums, curve = {}, None
    returned = []
    for call, (held, across, _) in enumerate(CALLS):
        count = jnp.where(variant == 0, counts[call][0], counts[call][1]).astype(jnp.int32)
        meta = jnp.stack([variant, count])
        names = [("x", c) for c in held] + [("y", c) for c in across]
        if call == 3:
            curve = after(curve, *returned[:2])
        parts, curve = run_tiles(
            jnp.asarray(tables[call]), meta, scale, [rows[c] for c in held],
            [columns[c] for c in across], [sums.get(name) for name in names], curve,
        )
        sums.update(zip(names, parts))
        if call == 0:
            then = after(shard, curve)
            for c in (2, 3):
                columns[c] = lax.ppermute(then, BOTH, column_route(c))
        if call == 1:
            for c in (0, 1):
                returned.append(lax.ppermute(sums["y", c], BOTH, backward(column_route(c))))
        if call == 2:
            for c in (1, 2, 3):
                returned.append(lax.ppermute(sums["x", c], BOTH, backward(row_route(c))))
    for c in (2, 3):
        returned.append(lax.ppermute(sums["y", c], BOTH, backward(column_route(c))))

    classes = lax.broadcasted_iota(jnp.int32, (noise_levels.shape[0], noise_class.shape[0]), 0)
    noise_diag = jnp.sum(
        jnp.where(noise_class[None, :] == classes, noise_levels[:, None], 0.0), axis=0
    )
    own_noise = noise_diag[None, :] * targets
    norm = 0.5 * jnp.sum(targets * targets, axis=1)
    curvature = jnp.sum(curve, axis=1) + 0.5 * jnp.sum(targets * own_noise, axis=1)
    scalars = after(jnp.stack([norm, curvature]), *returned[2:5])

    own = sums["x", 0]
    for part in returned:
        own = own + part
    scalars, own = summed_over_devices(scalars, own)
    step_size = scalars[0] / scalars[1]
    image = own + lax.ppermute(own, "grp", [(0, 1), (1, 0)]) + own_noise
    return (step_size[:, None] * targets, targets - step_size[:, None] * image)


def solution(mesh):
    return jax.shard_map(
        on_device,
        mesh=mesh,
        in_specs=(P(None, "blk"), P(None, "blk"), P(), P(), P("blk")),
        out_specs=(P(None, "blk"), P(None, "blk")),
        check_vma=False,
    )
```

```python
import functools
import math

import jax
import jax.numpy as jnp
import numpy as np
from jax import lax
from jax.experimental import pallas as pl
from jax.experimental.pallas import tpu as pltpu
from jax.sharding import PartitionSpec as P

BOTH = ("blk", "grp")
SHARD = 1536
ROWS = 24
CHUNKS = 4
SUPER = SHARD * CHUNKS
NSUPER = 16
NVEC = 16
TILE = 768
SUB = 256
LOG2E = math.log2(math.e)
SHIFT = 1.5 * LOG2E
OFFSET = 0.75 * LOG2E * LOG2E
FACTOR = 2.0**SHIFT / (3.0 * LOG2E * LOG2E)
bf16 = jnp.bfloat16
f32 = jnp.float32
f8 = jnp.float8_e5m2


def device_at(block, member):
    return (CHUNKS * block + member // 2) * 2 + member % 2


def column_route(chunk):
    route = []
    for a in range(NSUPER):
        for d in range(8):
            source = (a + (d if d else 8)) % NSUPER
            member = ((d // 2) ^ chunk) * 2 + d % 2
            route.append((device_at(source, member), device_at(a, d)))
    return route


def row_route(chunk):
    return [
        (device_at(a, ((d // 2) ^ chunk) * 2 + d % 2), device_at(a, d))
        for a in range(NSUPER)
        for d in range(8)
    ]


def block_route():
    return [
        (device_at((a + (d if d else 8)) % NSUPER, d), device_at(a, d))
        for a in range(NSUPER)
        for d in range(8)
    ]


def backward(route):
    return [(b, a) for a, b in route]


CALLS = [
    ((0, 1), (0,), [(0, 0), (1, 0)]),
    ((2, 3), (0,), [(2, 0), (3, 0)]),
    ((0, 1, 2, 3), (1,), [(0, 1), (1, 1), (2, 1), (3, 1)]),
    ((0, 1, 2, 3), (2, 3), [(i, j) for i in (1, 2, 3) for j in (2, 3)]),
    ((0,), (2, 3), [(0, 2), (0, 3)]),
]
OFF = [(1, 0), (2, 1), (3, 1), (0, 2), (0, 3), (2, 3)]
ON = [[(0, 0), (1, 1)], [(2, 2), (3, 3)]]
FILL = [[0, 8, 4, 20, 0], [4, 8, 8, 12, 0]]
PER = SHARD // TILE
GIVEN = [(0, 3 * PER), (1, 3 * PER), (0, 3 * PER + 1), (1, 3 * PER + 1)]


def tile_tables():
    side = SUPER // TILE
    triangles = [
        [(i, j) for j in range(side) for i in range(j + 1) if (i, j) not in GIVEN] for _ in range(2)
    ]
    tables, counts = [], []
    for call, (held, columns, pairs) in enumerate(CALLS):

        def at(i, k=0):
            return held.index((i // PER) ^ k) * PER + i % PER

        def pair(i, j):
            first = (len(held) + columns.index(j)) * PER
            return [(at(i * PER + y), first + x, 1) for y in range(PER) for x in range(PER)]

        regular = [t for i, j in pairs for t in pair(i, j)]
        lists = [regular]
        for half in range(2):
            tiles = [t for i, j in OFF + ON[half] if (i, j) in pairs for t in pair(i, j)]
            fits = [t for t in triangles[half] if all(i // PER in held for i in t)]
            part = fits[: FILL[half][call]]
            assert len(part) == FILL[half][call]
            triangles[half] = [t for t in triangles[half] if t not in part]
            tiles += [(at(i), at(j), int(i != j)) for i, j in part]
            lists.append(tiles)
        given = GIVEN if call == 3 else []
        lists.append(regular + [(at(i), at(j), 1) for i, j in given[:2]])
        lists.append(regular + [(at(i, 1), at(j, 1), 1) for i, j in given[2:]])
        longest = max(len(x) for x in lists)
        counts.append(np.array([len(x) for x in lists], np.int32))
        assert all(len(x) % 2 == 0 for x in lists)
        tables.append(
            np.array(
                [
                    [(i * TILE, j * TILE, k) for i, j, k in x + x[:1] * (longest - len(x))]
                    for x in lists
                ],
                np.int32,
            )
        )
    assert triangles == [[], []]
    return tables, counts


def pieces(value, count, dtype=bf16):
    out = []
    for _ in range(count):
        piece = value.astype(dtype).astype(f32)
        out.append(piece)
        value = value - piece
    return out


def kernel_values(squared):
    squared = jnp.maximum(squared, 1e-12)
    shifted = -SHIFT - squared * lax.rsqrt(squared)
    return (shifted * shifted + OFFSET) * jnp.exp2(shifted)


def tile_kernel(x_count, places, begun, *refs):
    refs = list(refs)
    table, meta, scale = refs[:3]
    every = len(places)
    given = 1 + max(array for array, _ in places)
    chunks = [refs[3 + array].at[pl.ds(ROWS * i, ROWS)] for array, i in places]
    rest = refs[3 + given :]
    sums_in, rest = dict(zip(begun, rest)), rest[len(begun) :]
    if begun:
        curve_in, rest = rest[0], rest[1:]
    sums_out, rest = rest[:every], rest[every:]
    curve_out, row_feat, col_feat, vectors, vectors8, row_sum, col_sum, hi0, hi1, lo0, lo1 = rest

    largest = jnp.full((NVEC, 1), 1e-30, f32)
    for chunk in chunks:
        part = jnp.max(jnp.abs(chunk[3:19, :]), axis=1, keepdims=True)
        largest = jnp.maximum(largest, part)
    upward = 1024.0 / largest
    downward = largest * (FACTOR / 1024.0)

    for place, chunk in enumerate(chunks):
        span = slice(place * SHARD, (place + 1) * SHARD)
        scaled = jnp.concatenate(
            [(chunk[c : c + 1, :] - 4.0) * scale[c] for c in range(3)], axis=0
        )
        a1, a2, a3 = pieces(scaled, 3)
        norm = jnp.sum(scaled * scaled, axis=0, keepdims=True)
        n1, n2, n3 = pieces(norm, 3)
        one = jnp.ones_like(norm)
        pad = jnp.zeros((8, SHARD), f32)
        columns = jnp.concatenate(
            [-2.0 * a1, -2.0 * a2, -2.0 * a1, -2.0 * a3, -2.0 * a2, -2.0 * a1,
             one, one, one, n1, n2, n3, pad], axis=0)
        col_feat[:, span] = columns.astype(bf16)
        vec = chunk[3:19, :] * upward
        vectors[:, span] = jnp.concatenate(pieces(vec, 2), axis=0).astype(bf16)
        vectors8[:, span] = jnp.concatenate(pieces(vec, 2, f8), axis=0).astype(f8)
        if place < x_count:
            rows = jnp.concatenate(
                [a1, a1, a2, a1, a2, a3, n1, n2, n3, one, one, one, pad], axis=0
            )
            row_feat[span, :] = jnp.transpose(rows).astype(bf16)
    for ref in (row_sum, col_sum, hi1, lo1):
        ref[...] = jnp.zeros_like(ref)
    variant = meta[0]
    count = meta[1]

    def place_of(t):
        return (
            pl.multiple_of(table[variant, t, 0], TILE),
            pl.multiple_of(table[variant, t, 1], TILE),
            table[variant, t, 2],
        )

    def produce(place, hi, lo, x, y):
        row, col, _ = place
        right = col_feat[:, pl.ds(pl.multiple_of(col + x, SUB), SUB)]
        left = row_feat[pl.ds(pl.multiple_of(row + y, SUB), SUB), :]
        value = kernel_values(jnp.dot(left, right, preferred_element_type=f32))
        high = value.astype(bf16)
        hi[y : y + SUB, x : x + SUB] = high
        lo[y : y + SUB, x : x + SUB] = (value - high.astype(f32)).astype(f8)

    def consume_rows(place, hi, lo, y):
        row, col, _ = place
        across = (((1,), (1,)), ((), ()))
        far = pl.ds(col, TILE)
        high, low = hi[y : y + SUB, :], lo[y : y + SUB, :]
        part = lax.dot_general(vectors[:, far], high, across, preferred_element_type=f32)
        part = part + lax.dot_general(vectors8[:, far], low, across, preferred_element_type=f32)
        row_sum[:, pl.ds(pl.multiple_of(row + y, SUB), SUB)] += part

    def consume_columns(place, hi, lo, x):
        row, col, keep = place
        near = pl.ds(row, TILE)
        high, low = hi[:, x : x + SUB], lo[:, x : x + SUB]
        part = jnp.dot(vectors[:, near], high, preferred_element_type=f32)
        part = part + jnp.dot(vectors8[:, near], low, preferred_element_type=f32)
        col_sum[:, pl.ds(pl.multiple_of(col + x, SUB), SUB)] += part * keep.astype(f32)

    def both(ahead, ahead_hi, ahead_lo, now, hi, lo):
        subs = [(x, y) for x in range(0, TILE, SUB) for y in range(0, TILE, SUB)]
        work = [(consume_rows, y) for y in range(0, TILE, SUB)]
        work += [(consume_columns, x) for x in range(0, TILE, SUB)]
        done = 0
        for n, (x, y) in enumerate(subs):
            if ahead is not None:
                produce(ahead, ahead_hi, ahead_lo, x, y)
            while done * len(subs) < (n + 1) * len(work) and done < len(work):
                step, offset = work[done]
                step(now, hi, lo, offset)
                done += 1

    def two_tiles(u, carried):
        both(place_of(2 * u), hi0, lo0, place_of(jnp.maximum(2 * u - 1, 0)), hi1, lo1)
        both(place_of(2 * u + 1), hi1, lo1, place_of(2 * u), hi0, lo0)
        return carried

    lax.fori_loop(0, count // 2, two_tiles, 0)
    both(None, None, None, place_of(count - 1), hi1, lo1)

    curve = curve_in[...] if begun else jnp.zeros((NVEC, 128), f32)
    for place, chunk in enumerate(chunks):
        span = slice(place * SHARD, (place + 1) * SHARD)
        total = col_sum[:, span]
        if place < x_count:
            total = total + row_sum[:, span]
        total = downward * (total[:NVEC] + total[NVEC:])
        product = total * chunk[3:19, :]
        for lane in range(0, SHARD, 128):
            curve = curve + product[:, lane : lane + 128]
        if place in sums_in:
            total = total + sums_in[place][...]
        sums_out[place][...] = total
    curve_out[...] = curve


def run_tiles(table, meta, scale, rows, columns, sums, curve):
    vmem = pl.BlockSpec(memory_space=pltpu.VMEM)
    smem = pl.BlockSpec(memory_space=pltpu.SMEM)
    count = len(rows) + len(columns)
    wide = len(rows) * SHARD
    every = count * SHARD
    arrays, places = [], []
    for array, i in [*rows, *columns]:
        found = [n for n, other in enumerate(arrays) if other is array]
        if not found:
            arrays.append(array)
        places.append((found[0] if found else len(arrays) - 1, i))
    begun = tuple(i for i, part in enumerate(sums) if part is not None)
    passed = [*arrays, *(sums[i] for i in begun)]
    if begun:
        passed.append(curve)
    out = pl.pallas_call(
        functools.partial(tile_kernel, len(rows), places, begun),
        out_shape=[jax.ShapeDtypeStruct((NVEC, SHARD), f32)] * count
        + [jax.ShapeDtypeStruct((NVEC, 128), f32)],
        in_specs=[smem] * 3 + [vmem] * len(passed),
        out_specs=[vmem] * (count + 1),
        scratch_shapes=[
            pltpu.VMEM((wide, 32), bf16),
            pltpu.VMEM((32, every), bf16),
            pltpu.VMEM((32, every), bf16),
            pltpu.VMEM((32, every), f8),
            pltpu.VMEM((32, wide), f32),
            pltpu.VMEM((32, every), f32),
        ]
        + [pltpu.VMEM((TILE, TILE), bf16)] * 2
        + [pltpu.VMEM((TILE, TILE), f8)] * 2,
        compiler_params=pltpu.CompilerParams(vmem_limit_bytes=48 * 2**20),
        cost_estimate=pl.CostEstimate(
            flops=1_500_000_000 * table.shape[1], bytes_accessed=2_000_000, transcendentals=0
        ),
    )(table, meta, scale, *passed)
    return out[:count], out[count]


def after(value, *others):
    return lax.optimization_barrier((value, *others))[0]


def on_device(points, targets, length_scales, noise_levels, noise_class):
    shard = jnp.concatenate([points, targets, jnp.zeros((ROWS - 19, SHARD), f32)], axis=0)
    first_column = lax.ppermute(shard, BOTH, column_route(0))
    partner = lax.ppermute(shard, "blk", [(i, i ^ 1) for i in range(64)])
    chip = jnp.concatenate([shard, partner], axis=0)
    beside = lax.ppermute(chip, "blk", [(i, i ^ 2) for i in range(64)])
    rows = {0: (shard, 0), 1: (partner, 0), 2: (beside, 0), 3: (beside, 1)}
    columns = {0: (first_column, 0)}

    block = lax.axis_index("blk")
    member = (block % CHUNKS) * 2 + lax.axis_index("grp")
    variant = jnp.where(member == 0, jnp.where(block < 32, 1, 2), 0)
    variant = jnp.where(member == 1, 3, jnp.where(member == 2, 4, variant)).astype(jnp.int32)
    tables, counts = tile_tables()
    scale = (math.sqrt(5.0) * LOG2E) / length_scales

    sums, curve = {}, None
    returned = []
    for call, (held, across, _) in enumerate(CALLS):
        meta = jnp.stack([variant, jnp.asarray(counts[call])[variant]])
        names = [("x", c) for c in held] + [("y", c) for c in across]
        parts, curve = run_tiles(
            jnp.asarray(tables[call]), meta, scale, [rows[c] for c in held],
            [columns[c] for c in across], [sums.get(name) for name in names], curve,
        )
        sums.update(zip(names, parts))
        if call == 0:
            others = after(jnp.concatenate([partner, beside], axis=0), curve)
            others = lax.ppermute(others, BOTH, block_route())
            columns.update({c: (others, c - 1) for c in (1, 2, 3)})
        if call == 3:
            for c in (0, 1):
                part = after(sums["y", c], curve)
                returned.append(lax.ppermute(part, BOTH, backward(column_route(c))))
            for c in (1, 2, 3):
                returned.append(lax.ppermute(sums["x", c], BOTH, backward(row_route(c))))
    for c in (2, 3):
        returned.append(lax.ppermute(sums["y", c], BOTH, backward(column_route(c))))

    classes = lax.broadcasted_iota(jnp.int32, (noise_levels.shape[0], noise_class.shape[0]), 0)
    noise_diag = jnp.sum(
        jnp.where(noise_class[None, :] == classes, noise_levels[:, None], 0.0), axis=0
    )
    own_noise = noise_diag[None, :] * targets
    norm = 0.5 * jnp.sum(targets * targets, axis=1)
    curvature = jnp.sum(curve, axis=1) + 0.5 * jnp.sum(targets * own_noise, axis=1)
    scalars = after(jnp.concatenate([norm, curvature]), *returned[:5])
    blocks = lax.axis_size("blk")
    scalars = lax.all_to_all(
        jnp.broadcast_to(scalars[None], (blocks, 2 * NVEC)), "blk", 0, 0, tiled=True
    )
    scalars = jnp.sum(scalars, axis=0)

    scalars, *returned = lax.optimization_barrier((scalars, *returned))
    own = sums["x", 0]
    for part in returned:
        own = own + part
    theirs = lax.ppermute(own, "grp", [(0, 1), (1, 0)])
    scalars = scalars + lax.ppermute(scalars, "grp", [(0, 1), (1, 0)])
    step_size = scalars[:NVEC] / scalars[NVEC:]
    image = own + theirs + own_noise
    return (step_size[:, None] * targets, targets - step_size[:, None] * image)


def solution(mesh):
    return jax.shard_map(
        on_device,
        mesh=mesh,
        in_specs=(P(None, "blk"), P(None, "blk"), P(), P(), P("blk")),
        out_specs=(P(None, "blk"), P(None, "blk")),
        check_vma=False,
    )
```

```python
import functools
import math

import jax
import jax.numpy as jnp
import numpy as np
from jax import lax
from jax.experimental import pallas as pl
from jax.experimental.pallas import tpu as pltpu
from jax.sharding import PartitionSpec as P

BOTH = ("blk", "grp")
SHARD = 1536
ROWS = 24
CHUNKS = 4
SUPER = SHARD * CHUNKS
NSUPER = 16
NVEC = 16
TILE = 768
SUB = 256
LOG2E = math.log2(math.e)
SHIFT = 1.5 * LOG2E
OFFSET = 0.75 * LOG2E * LOG2E
FACTOR = 2.0**SHIFT / (3.0 * LOG2E * LOG2E)
bf16 = jnp.bfloat16
f32 = jnp.float32
f8 = jnp.float8_e5m2


def device_at(block, member):
    return (CHUNKS * block + member // 2) * 2 + member % 2


DISTANCE = [8 - 2 * (m // 2) if m % 2 == 0 else 7 - 2 * ((m // 2) ^ 2) for m in range(8)]


def column_source(a, m):
    s = (a + DISTANCE[m]) % NSUPER
    k, g = m // 2, m % 2
    k ^= 2 * ((a ^ s) & 1)
    even = 8 - 2 * k
    crosses = [s % 8 < even, s % 8 < even - 1]
    return s, k, g ^ (crosses[0] and crosses[1])


def column_route(chunk):
    route = []
    for a in range(NSUPER):
        for m in range(8):
            s, k, g = column_source(a, m)
            route.append((device_at(s, 2 * (k ^ chunk) + g), device_at(a, m)))
    assert len({x for x, _ in route}) == len({x for _, x in route}) == 128
    return route


def row_route(chunk):
    return [
        (device_at(a, ((d // 2) ^ chunk) * 2 + d % 2), device_at(a, d))
        for a in range(NSUPER)
        for d in range(8)
    ]


def backward(route):
    return [(b, a) for a, b in route]


CALLS = [
    ((0, 1, 2, 3), (0,), [(i, 0) for i in range(4)]),
    ((0, 1, 2, 3), (1, 2, 3), [(i, j) for j in (1, 2, 3) for i in range(4)]),
]
OFF = [(1, 0), (2, 1), (3, 1), (0, 2), (0, 3), (2, 3)]
ON = [[(0, 0), (1, 1)], [(2, 2), (3, 3)]]
FILL = [[8, 24], [12, 20]]
PER = SHARD // TILE
GIVEN = [(0, 3 * PER), (1, 3 * PER), (0, 3 * PER + 1), (1, 3 * PER + 1)]


def tile_tables():
    side = SUPER // TILE
    triangles = [
        [(i, j) for j in range(side) for i in range(j + 1) if (i, j) not in GIVEN] for _ in range(2)
    ]
    tables, counts = [], []
    for call, (held, columns, pairs) in enumerate(CALLS):

        def at(i, k=0):
            return held.index((i // PER) ^ k) * PER + i % PER

        def pair(i, j):
            first = (len(held) + columns.index(j)) * PER
            return [(at(i * PER + y), first + x, 1) for y in range(PER) for x in range(PER)]

        regular = [t for i, j in pairs for t in pair(i, j)]
        lists = [regular]
        for half in range(2):
            tiles = [t for i, j in OFF + ON[half] if (i, j) in pairs for t in pair(i, j)]
            fits = [t for t in triangles[half] if all(i // PER in held for i in t)]
            part = fits[: FILL[half][call]]
            assert len(part) == FILL[half][call]
            triangles[half] = [t for t in triangles[half] if t not in part]
            tiles += [(at(i), at(j), int(i != j)) for i, j in part]
            lists.append(tiles)
        given = GIVEN if call == 1 else []
        lists.append(regular + [(at(i), at(j), 1) for i, j in given[:2]])
        lists.append(regular + [(at(i, 1), at(j, 1), 1) for i, j in given[2:]])
        longest = max(len(x) for x in lists)
        counts.append(np.array([len(x) for x in lists], np.int32))
        assert all(len(x) % 2 == 0 for x in lists)
        tables.append(
            np.array(
                [
                    [(i * TILE, j * TILE, k) for i, j, k in x + x[:1] * (longest - len(x))]
                    for x in lists
                ],
                np.int32,
            )
        )
    assert triangles == [[], []]
    return tables, counts


def pieces(value, count, dtype=bf16):
    out = []
    for _ in range(count):
        piece = value.astype(dtype).astype(f32)
        out.append(piece)
        value = value - piece
    return out


def kernel_values(squared):
    squared = jnp.maximum(squared, 1e-12)
    shifted = -SHIFT - squared * lax.rsqrt(squared)
    return (shifted * shifted + OFFSET) * jnp.exp2(shifted)


def tile_kernel(x_count, places, begun, *refs):
    refs = list(refs)
    table, meta, scale = refs[:3]
    every = len(places)
    given = 1 + max(array for array, _ in places)
    chunks = [refs[3 + array].at[pl.ds(ROWS * i, ROWS)] for array, i in places]
    rest = refs[3 + given :]
    sums_in, rest = dict(zip(begun, rest)), rest[len(begun) :]
    if begun:
        curve_in, rest = rest[0], rest[1:]
    sums_out, rest = rest[:every], rest[every:]
    curve_out, row_feat, col_feat, vectors, vectors8, row_sum, col_sum, hi0, hi1, lo0, lo1 = rest

    largest = jnp.full((NVEC, 1), 1e-30, f32)
    for chunk in chunks:
        part = jnp.max(jnp.abs(chunk[3:19, :]), axis=1, keepdims=True)
        largest = jnp.maximum(largest, part)
    upward = 1024.0 / largest
    downward = largest * (FACTOR / 1024.0)

    for place, chunk in enumerate(chunks):
        span = slice(place * SHARD, (place + 1) * SHARD)
        scaled = jnp.concatenate(
            [(chunk[c : c + 1, :] - 4.0) * scale[c] for c in range(3)], axis=0
        )
        a1, a2, a3 = pieces(scaled, 3)
        norm = jnp.sum(scaled * scaled, axis=0, keepdims=True)
        n1, n2, n3 = pieces(norm, 3)
        one = jnp.ones_like(norm)
        pad = jnp.zeros((8, SHARD), f32)
        columns = jnp.concatenate(
            [-2.0 * a1, -2.0 * a2, -2.0 * a1, -2.0 * a3, -2.0 * a2, -2.0 * a1,
             one, one, one, n1, n2, n3, pad], axis=0)
        col_feat[:, span] = columns.astype(bf16)
        vec = chunk[3:19, :] * upward
        vectors[:, span] = jnp.concatenate(pieces(vec, 2), axis=0).astype(bf16)
        vectors8[:, span] = jnp.concatenate(pieces(vec, 2, f8), axis=0).astype(f8)
        if place < x_count:
            rows = jnp.concatenate(
                [a1, a1, a2, a1, a2, a3, n1, n2, n3, one, one, one, pad], axis=0
            )
            row_feat[span, :] = jnp.transpose(rows).astype(bf16)
    for ref in (row_sum, col_sum, hi1, lo1):
        ref[...] = jnp.zeros_like(ref)
    variant = meta[0]
    count = meta[1]

    def place_of(t):
        return (
            pl.multiple_of(table[variant, t, 0], TILE),
            pl.multiple_of(table[variant, t, 1], TILE),
            table[variant, t, 2],
        )

    def produce(place, hi, lo, x, y):
        row, col, _ = place
        right = col_feat[:, pl.ds(pl.multiple_of(col + x, SUB), SUB)]
        left = row_feat[pl.ds(pl.multiple_of(row + y, SUB), SUB), :]
        value = kernel_values(jnp.dot(left, right, preferred_element_type=f32))
        high = value.astype(bf16)
        hi[y : y + SUB, x : x + SUB] = high
        lo[y : y + SUB, x : x + SUB] = (value - high.astype(f32)).astype(f8)

    def consume_rows(place, hi, lo, y):
        row, col, _ = place
        across = (((1,), (1,)), ((), ()))
        far = pl.ds(col, TILE)
        high, low = hi[y : y + SUB, :], lo[y : y + SUB, :]
        part = lax.dot_general(vectors[:, far], high, across, preferred_element_type=f32)
        part = part + lax.dot_general(vectors8[:, far], low, across, preferred_element_type=f32)
        row_sum[:, pl.ds(pl.multiple_of(row + y, SUB), SUB)] += part

    def consume_columns(place, hi, lo, x):
        row, col, keep = place
        near = pl.ds(row, TILE)
        high, low = hi[:, x : x + SUB], lo[:, x : x + SUB]
        part = jnp.dot(vectors[:, near], high, preferred_element_type=f32)
        part = part + jnp.dot(vectors8[:, near], low, preferred_element_type=f32)
        col_sum[:, pl.ds(pl.multiple_of(col + x, SUB), SUB)] += part * keep.astype(f32)

    def both(ahead, ahead_hi, ahead_lo, now, hi, lo):
        subs = [(x, y) for x in range(0, TILE, SUB) for y in range(0, TILE, SUB)]
        work = [(consume_rows, y) for y in range(0, TILE, SUB)]
        work += [(consume_columns, x) for x in range(0, TILE, SUB)]
        done = 0
        for n, (x, y) in enumerate(subs):
            if ahead is not None:
                produce(ahead, ahead_hi, ahead_lo, x, y)
            while done * len(subs) < (n + 1) * len(work) and done < len(work):
                step, offset = work[done]
                step(now, hi, lo, offset)
                done += 1

    def two_tiles(u, carried):
        both(place_of(2 * u), hi0, lo0, place_of(jnp.maximum(2 * u - 1, 0)), hi1, lo1)
        both(place_of(2 * u + 1), hi1, lo1, place_of(2 * u), hi0, lo0)
        return carried

    lax.fori_loop(0, count // 2, two_tiles, 0)
    both(None, None, None, place_of(count - 1), hi1, lo1)

    curve = curve_in[...] if begun else jnp.zeros((NVEC, 128), f32)
    for place, chunk in enumerate(chunks):
        span = slice(place * SHARD, (place + 1) * SHARD)
        total = col_sum[:, span]
        if place < x_count:
            total = total + row_sum[:, span]
        total = downward * (total[:NVEC] + total[NVEC:])
        product = total * chunk[3:19, :]
        for lane in range(0, SHARD, 128):
            curve = curve + product[:, lane : lane + 128]
        if place in sums_in:
            total = total + sums_in[place][...]
        sums_out[place][...] = total
    curve_out[...] = curve


def run_tiles(table, meta, scale, rows, columns, sums, curve):
    vmem = pl.BlockSpec(memory_space=pltpu.VMEM)
    smem = pl.BlockSpec(memory_space=pltpu.SMEM)
    count = len(rows) + len(columns)
    wide = len(rows) * SHARD
    every = count * SHARD
    arrays, places = [], []
    for array, i in [*rows, *columns]:
        found = [n for n, other in enumerate(arrays) if other is array]
        if not found:
            arrays.append(array)
        places.append((found[0] if found else len(arrays) - 1, i))
    begun = tuple(i for i, part in enumerate(sums) if part is not None)
    passed = [*arrays, *(sums[i] for i in begun)]
    if begun:
        passed.append(curve)
    out = pl.pallas_call(
        functools.partial(tile_kernel, len(rows), places, begun),
        out_shape=[jax.ShapeDtypeStruct((NVEC, SHARD), f32)] * count
        + [jax.ShapeDtypeStruct((NVEC, 128), f32)],
        in_specs=[smem] * 3 + [vmem] * len(passed),
        out_specs=[vmem] * (count + 1),
        scratch_shapes=[
            pltpu.VMEM((wide, 32), bf16),
            pltpu.VMEM((32, every), bf16),
            pltpu.VMEM((32, every), bf16),
            pltpu.VMEM((32, every), f8),
            pltpu.VMEM((32, wide), f32),
            pltpu.VMEM((32, every), f32),
        ]
        + [pltpu.VMEM((TILE, TILE), bf16)] * 2
        + [pltpu.VMEM((TILE, TILE), f8)] * 2,
        compiler_params=pltpu.CompilerParams(vmem_limit_bytes=48 * 2**20),
        cost_estimate=pl.CostEstimate(
            flops=1_500_000_000 * table.shape[1], bytes_accessed=2_000_000, transcendentals=0
        ),
    )(table, meta, scale, *passed)
    return out[:count], out[count]


def after(value, *others):
    return lax.optimization_barrier((value, *others))[0]


def on_device(points, targets, length_scales, noise_levels, noise_class):
    shard = jnp.concatenate([points, targets, jnp.zeros((ROWS - 19, SHARD), f32)], axis=0)
    swap = [(i, i ^ 1) for i in range(64)]
    first_column = lax.ppermute(shard, BOTH, column_route(0))
    beside = lax.ppermute(shard, "blk", [(i, i ^ 2) for i in range(64)])
    partner = lax.ppermute(shard, "blk", swap)
    across = lax.ppermute(beside, "blk", swap)
    rest = jnp.concatenate([partner, beside, across], axis=0)
    others = lax.ppermute(rest, BOTH, column_route(0))
    rows = {0: (shard, 0), 1: (rest, 0), 2: (rest, 1), 3: (rest, 2)}
    columns = {0: (first_column, 0), 1: (others, 0), 2: (others, 1), 3: (others, 2)}

    block = lax.axis_index("blk")
    member = (block % CHUNKS) * 2 + lax.axis_index("grp")
    variant = jnp.where(member == 0, jnp.where(block < 32, 1, 2), 0)
    variant = jnp.where(member == 1, 3, jnp.where(member == 2, 4, variant)).astype(jnp.int32)
    tables, counts = tile_tables()
    scale = (math.sqrt(5.0) * LOG2E) / length_scales

    def sent_back(name):
        kind, c = name
        route = row_route(c) if kind == "x" else column_route(c)
        return lax.ppermute(sums[name], BOTH, backward(route))

    sums, curve = {}, None
    returned = []
    for call, (held, across, _) in enumerate(CALLS):
        meta = jnp.stack([variant, jnp.asarray(counts[call])[variant]])
        names = [("x", c) for c in held] + [("y", c) for c in across]
        parts, curve = run_tiles(
            jnp.asarray(tables[call]), meta, scale, [rows[c] for c in held],
            [columns[c] for c in across], [sums.get(name) for name in names], curve,
        )
        sums.update(zip(names, parts))
        done = [[("y", 0)], [("y", 1), ("y", 2), ("y", 3), ("x", 1), ("x", 2), ("x", 3)]]
        returned += [sent_back(name) for name in done[call]]

    classes = lax.broadcasted_iota(jnp.int32, (noise_levels.shape[0], noise_class.shape[0]), 0)
    noise_diag = jnp.sum(
        jnp.where(noise_class[None, :] == classes, noise_levels[:, None], 0.0), axis=0
    )
    own_noise = noise_diag[None, :] * targets
    norm = 0.5 * jnp.sum(targets * targets, axis=1)
    curvature = jnp.sum(curve, axis=1) + 0.5 * jnp.sum(targets * own_noise, axis=1)
    scalars = after(jnp.concatenate([norm, curvature]), *returned[:1])
    blocks = lax.axis_size("blk")
    scalars = lax.all_to_all(
        jnp.broadcast_to(scalars[None], (blocks, 2 * NVEC)), "blk", 0, 0, tiled=True
    )
    scalars = jnp.sum(scalars, axis=0)

    scalars, *returned = lax.optimization_barrier((scalars, *returned))
    own = sums["x", 0]
    for part in returned:
        own = own + part
    theirs = lax.ppermute(own, "grp", [(0, 1), (1, 0)])
    scalars = scalars + lax.ppermute(scalars, "grp", [(0, 1), (1, 0)])
    step_size = scalars[:NVEC] / scalars[NVEC:]
    image = own + theirs + own_noise
    return (step_size[:, None] * targets, targets - step_size[:, None] * image)


def solution(mesh):
    return jax.shard_map(
        on_device,
        mesh=mesh,
        in_specs=(P(None, "blk"), P(None, "blk"), P(), P(), P("blk")),
        out_specs=(P(None, "blk"), P(None, "blk")),
        check_vma=False,
    )
```

```python
import functools
import math

import jax
import jax.numpy as jnp
import numpy as np
from jax import lax
from jax.experimental import pallas as pl
from jax.experimental.pallas import tpu as pltpu
from jax.sharding import PartitionSpec as P

BOTH = ("blk", "grp")
SHARD = 1536
ROWS = 24
CHUNKS = 4
SUPER = SHARD * CHUNKS
NSUPER = 16
NVEC = 16
TILE = 768
SUB = 256
LOG2E = math.log2(math.e)
SHIFT = 1.5 * LOG2E
OFFSET = 0.75 * LOG2E * LOG2E
FACTOR = 2.0**SHIFT / (3.0 * LOG2E * LOG2E)
bf16 = jnp.bfloat16
f32 = jnp.float32
f8 = jnp.float8_e5m2


def device_at(block, member):
    return (CHUNKS * block + member // 2) * 2 + member % 2


DISTANCE = [8 - 2 * (m // 2) if m % 2 == 0 else 7 - 2 * ((m // 2) ^ 2) for m in range(8)]


def column_source(a, m):
    s = (a + DISTANCE[m]) % NSUPER
    k, g = m // 2, m % 2
    k ^= 2 * ((a ^ s) & 1)
    even = 8 - 2 * k
    crosses = [s % 8 < even, s % 8 < even - 1]
    return s, k, g ^ (crosses[0] and crosses[1])


def column_route(chunk):
    route = []
    for a in range(NSUPER):
        for m in range(8):
            s, k, g = column_source(a, m)
            route.append((device_at(s, 2 * (k ^ chunk) + g), device_at(a, m)))
    assert len({x for x, _ in route}) == len({x for _, x in route}) == 128
    return route


def row_route(chunk):
    return [
        (device_at(a, ((d // 2) ^ chunk) * 2 + d % 2), device_at(a, d))
        for a in range(NSUPER)
        for d in range(8)
    ]


def backward(route):
    return [(b, a) for a, b in route]


CALLS = [
    ((0, 1, 2, 3), (0,), [(i, 0) for i in range(4)]),
    ((0, 1, 2, 3), (1, 2, 3), [(i, j) for j in (1, 2, 3) for i in range(4)]),
]
OFF = [(1, 0), (2, 1), (3, 1), (0, 2), (0, 3), (2, 3)]
ON = [[(0, 0), (1, 1)], [(2, 2), (3, 3)]]
FILL = [[8, 24], [12, 20]]
PER = SHARD // TILE
GIVEN = [(0, 3 * PER), (1, 3 * PER), (0, 3 * PER + 1), (1, 3 * PER + 1)]


def tile_tables():
    side = SUPER // TILE
    triangles = [
        [(i, j) for j in range(side) for i in range(j + 1) if (i, j) not in GIVEN] for _ in range(2)
    ]
    tables, counts = [], []
    for call, (held, columns, pairs) in enumerate(CALLS):

        def at(i, k=0):
            return held.index((i // PER) ^ k) * PER + i % PER

        def pair(i, j):
            first = (len(held) + columns.index(j)) * PER
            return [(at(i * PER + y), first + x, 1) for y in range(PER) for x in range(PER)]

        regular = [t for i, j in pairs for t in pair(i, j)]
        lists = [regular]
        for half in range(2):
            tiles = [t for i, j in OFF + ON[half] if (i, j) in pairs for t in pair(i, j)]
            fits = [t for t in triangles[half] if all(i // PER in held for i in t)]
            part = fits[: FILL[half][call]]
            assert len(part) == FILL[half][call]
            triangles[half] = [t for t in triangles[half] if t not in part]
            tiles += [(at(i), at(j), int(i != j)) for i, j in part]
            lists.append(tiles)
        given = GIVEN if call == 1 else []
        lists.append(regular + [(at(i), at(j), 1) for i, j in given[:2]])
        lists.append(regular + [(at(i, 1), at(j, 1), 1) for i, j in given[2:]])
        longest = max(len(x) for x in lists)
        counts.append(np.array([len(x) for x in lists], np.int32))
        assert all(len(x) % 2 == 0 for x in lists)
        tables.append(
            np.array(
                [
                    [(i * TILE, j * TILE, k) for i, j, k in x + x[:1] * (longest - len(x))]
                    for x in lists
                ],
                np.int32,
            )
        )
    assert triangles == [[], []]
    return tables, counts


def pieces(value, count, dtype=bf16):
    out = []
    for _ in range(count):
        piece = value.astype(dtype).astype(f32)
        out.append(piece)
        value = value - piece
    return out


def kernel_values(squared):
    squared = jnp.maximum(squared, 1e-12)
    shifted = -SHIFT - squared * lax.rsqrt(squared)
    return (shifted * shifted + OFFSET) * jnp.exp2(shifted)


def tile_kernel(x_count, places, begun, *refs):
    refs = list(refs)
    table, meta, scale = refs[:3]
    every = len(places)
    given = 1 + max(array for array, _ in places)
    chunks = [refs[3 + array].at[pl.ds(ROWS * i, ROWS)] for array, i in places]
    rest = refs[3 + given :]
    sums_in, rest = dict(zip(begun, rest)), rest[len(begun) :]
    if begun:
        curve_in, rest = rest[0], rest[1:]
    sums_out, rest = rest[:every], rest[every:]
    curve_out, row_feat, col_feat, vectors, vectors8, row_sum, col_sum, hi0, hi1, lo0, lo1 = rest

    largest = jnp.full((NVEC, 1), 1e-30, f32)
    for chunk in chunks:
        part = jnp.max(jnp.abs(chunk[3:19, :]), axis=1, keepdims=True)
        largest = jnp.maximum(largest, part)
    upward = 1024.0 / largest
    downward = largest * (FACTOR / 1024.0)

    for place, chunk in enumerate(chunks):
        span = slice(place * SHARD, (place + 1) * SHARD)
        scaled = jnp.concatenate(
            [(chunk[c : c + 1, :] - 4.0) * scale[c] for c in range(3)], axis=0
        )
        a1, a2, a3 = pieces(scaled, 3)
        norm = jnp.sum(scaled * scaled, axis=0, keepdims=True)
        n1, n2, n3 = pieces(norm, 3)
        one = jnp.ones_like(norm)
        pad = jnp.zeros((8, SHARD), f32)
        columns = jnp.concatenate(
            [-2.0 * a1, -2.0 * a2, -2.0 * a1, -2.0 * a3, -2.0 * a2, -2.0 * a1,
             one, one, one, n1, n2, n3, pad], axis=0)
        col_feat[:, span] = columns.astype(bf16)
        vec = chunk[3:19, :] * upward
        vectors[:, span] = jnp.concatenate(pieces(vec, 2), axis=0).astype(bf16)
        vectors8[:, span] = jnp.concatenate(pieces(vec, 2, f8), axis=0).astype(f8)
        if place < x_count:
            rows = jnp.concatenate(
                [a1, a1, a2, a1, a2, a3, n1, n2, n3, one, one, one, pad], axis=0
            )
            row_feat[span, :] = jnp.transpose(rows).astype(bf16)
    for ref in (row_sum, col_sum, hi1, lo1):
        ref[...] = jnp.zeros_like(ref)
    variant = meta[0]
    count = meta[1]

    def place_of(t):
        return (
            pl.multiple_of(table[variant, t, 0], TILE),
            pl.multiple_of(table[variant, t, 1], TILE),
            table[variant, t, 2],
        )

    def produce(place, hi, lo, x, y):
        row, col, _ = place
        right = col_feat[:, pl.ds(pl.multiple_of(col + x, SUB), SUB)]
        left = row_feat[pl.ds(pl.multiple_of(row + y, SUB), SUB), :]
        value = kernel_values(jnp.dot(left, right, preferred_element_type=f32))
        high = value.astype(bf16)
        hi[y : y + SUB, x : x + SUB] = high
        lo[y : y + SUB, x : x + SUB] = (value - high.astype(f32)).astype(f8)

    def consume_rows(place, hi, lo, y):
        row, col, _ = place
        across = (((1,), (1,)), ((), ()))
        far = pl.ds(col, TILE)
        high, low = hi[y : y + SUB, :], lo[y : y + SUB, :]
        part = lax.dot_general(vectors[:, far], high, across, preferred_element_type=f32)
        part = part + lax.dot_general(vectors8[:, far], low, across, preferred_element_type=f32)
        row_sum[:, pl.ds(pl.multiple_of(row + y, SUB), SUB)] += part

    def consume_columns(place, hi, lo, x):
        row, col, keep = place
        near = pl.ds(row, TILE)
        high, low = hi[:, x : x + SUB], lo[:, x : x + SUB]
        part = jnp.dot(vectors[:, near], high, preferred_element_type=f32)
        part = part + jnp.dot(vectors8[:, near], low, preferred_element_type=f32)
        col_sum[:, pl.ds(pl.multiple_of(col + x, SUB), SUB)] += part * keep.astype(f32)

    def both(ahead, ahead_hi, ahead_lo, now, hi, lo):
        subs = [(x, y) for x in range(0, TILE, SUB) for y in range(0, TILE, SUB)]
        work = [(consume_rows, y) for y in range(0, TILE, SUB)]
        work += [(consume_columns, x) for x in range(0, TILE, SUB)]
        done = 0
        for n, (x, y) in enumerate(subs):
            if ahead is not None:
                produce(ahead, ahead_hi, ahead_lo, x, y)
            while done * len(subs) < (n + 1) * len(work) and done < len(work):
                step, offset = work[done]
                step(now, hi, lo, offset)
                done += 1

    def two_tiles(u, carried):
        both(place_of(2 * u), hi0, lo0, place_of(jnp.maximum(2 * u - 1, 0)), hi1, lo1)
        both(place_of(2 * u + 1), hi1, lo1, place_of(2 * u), hi0, lo0)
        return carried

    lax.fori_loop(0, count // 2, two_tiles, 0)
    both(None, None, None, place_of(count - 1), hi1, lo1)

    curve = curve_in[...] if begun else jnp.zeros((NVEC, 128), f32)
    for place, chunk in enumerate(chunks):
        span = slice(place * SHARD, (place + 1) * SHARD)
        total = col_sum[:, span]
        if place < x_count:
            total = total + row_sum[:, span]
        total = downward * (total[:NVEC] + total[NVEC:])
        product = total * chunk[3:19, :]
        for lane in range(0, SHARD, 128):
            curve = curve + product[:, lane : lane + 128]
        if place in sums_in:
            total = total + sums_in[place][...]
        sums_out[place][...] = total
    curve_out[...] = curve


def run_tiles(table, meta, scale, rows, columns, sums, curve):
    vmem = pl.BlockSpec(memory_space=pltpu.VMEM)
    smem = pl.BlockSpec(memory_space=pltpu.SMEM)
    count = len(rows) + len(columns)
    wide = len(rows) * SHARD
    every = count * SHARD
    arrays, places = [], []
    for array, i in [*rows, *columns]:
        found = [n for n, other in enumerate(arrays) if other is array]
        if not found:
            arrays.append(array)
        places.append((found[0] if found else len(arrays) - 1, i))
    begun = tuple(i for i, part in enumerate(sums) if part is not None)
    passed = [*arrays, *(sums[i] for i in begun)]
    if begun:
        passed.append(curve)
    out = pl.pallas_call(
        functools.partial(tile_kernel, len(rows), places, begun),
        out_shape=[jax.ShapeDtypeStruct((NVEC, SHARD), f32)] * count
        + [jax.ShapeDtypeStruct((NVEC, 128), f32)],
        in_specs=[smem] * 3 + [vmem] * len(passed),
        out_specs=[vmem] * (count + 1),
        scratch_shapes=[
            pltpu.VMEM((wide, 32), bf16),
            pltpu.VMEM((32, every), bf16),
            pltpu.VMEM((32, every), bf16),
            pltpu.VMEM((32, every), f8),
            pltpu.VMEM((32, wide), f32),
            pltpu.VMEM((32, every), f32),
        ]
        + [pltpu.VMEM((TILE, TILE), bf16)] * 2
        + [pltpu.VMEM((TILE, TILE), f8)] * 2,
        compiler_params=pltpu.CompilerParams(vmem_limit_bytes=48 * 2**20),
        cost_estimate=pl.CostEstimate(
            flops=1_500_000_000 * table.shape[1], bytes_accessed=2_000_000, transcendentals=0
        ),
    )(table, meta, scale, *passed)
    return out[:count], out[count]


def after(value, *others):
    return lax.optimization_barrier((value, *others))[0]


def on_device(points, targets, length_scales, noise_levels, noise_class):
    shard = jnp.concatenate([points, targets, jnp.zeros((ROWS - 19, SHARD), f32)], axis=0)
    swap = [(i, i ^ 1) for i in range(64)]
    first_column = lax.ppermute(shard, BOTH, column_route(0))
    beside = lax.ppermute(shard, "blk", [(i, i ^ 2) for i in range(64)])
    partner = lax.ppermute(shard, "blk", swap)
    across = lax.ppermute(beside, "blk", swap)
    rest = jnp.concatenate([partner, beside, across], axis=0)
    others = lax.ppermute(rest, BOTH, column_route(0))
    rows = {0: (shard, 0), 1: (rest, 0), 2: (rest, 1), 3: (rest, 2)}
    columns = {0: (first_column, 0), 1: (others, 0), 2: (others, 1), 3: (others, 2)}

    block = lax.axis_index("blk")
    member = (block % CHUNKS) * 2 + lax.axis_index("grp")
    variant = jnp.where(member == 0, jnp.where(block < 32, 1, 2), 0)
    variant = jnp.where(member == 1, 3, jnp.where(member == 2, 4, variant)).astype(jnp.int32)
    tables, counts = tile_tables()
    scale = (math.sqrt(5.0) * LOG2E) / length_scales

    def sent_back(name):
        kind, c = name
        route = row_route(c) if kind == "x" else column_route(c)
        return lax.ppermute(sums[name], BOTH, backward(route))

    sums, curve = {}, None
    for call, (held, across, _) in enumerate(CALLS):
        meta = jnp.stack([variant, jnp.asarray(counts[call])[variant]])
        names = [("x", c) for c in held] + [("y", c) for c in across]
        parts, curve = run_tiles(
            jnp.asarray(tables[call]), meta, scale, [rows[c] for c in held],
            [columns[c] for c in across], [sums.get(name) for name in names], curve,
        )
        sums.update(zip(names, parts))

    column_sums = jnp.concatenate([sums["y", c] for c in range(CHUNKS)], axis=0)
    column_sums = lax.ppermute(column_sums, BOTH, backward(column_route(0)))

    classes = lax.broadcasted_iota(jnp.int32, (noise_levels.shape[0], noise_class.shape[0]), 0)
    noise_diag = jnp.sum(
        jnp.where(noise_class[None, :] == classes, noise_levels[:, None], 0.0), axis=0
    )
    own_noise = noise_diag[None, :] * targets
    norm = 0.5 * jnp.sum(targets * targets, axis=1)
    curvature = jnp.sum(curve, axis=1) + 0.5 * jnp.sum(targets * own_noise, axis=1)
    scalars = jnp.concatenate([norm, curvature])
    blocks = lax.axis_size("blk")
    scalars = lax.all_to_all(
        jnp.broadcast_to(scalars[None], (blocks, 2 * NVEC)), "blk", 0, 0, tiled=True
    )
    scalars = jnp.sum(scalars, axis=0)

    scalars, column_sums = lax.optimization_barrier((scalars, column_sums))
    total = [sums["x", c] + column_sums[c * NVEC : (c + 1) * NVEC] for c in range(CHUNKS)]
    pair = lax.ppermute(jnp.concatenate([total[1], total[3]], axis=0), "blk", swap)
    near = lax.ppermute(total[2] + pair[NVEC:], "blk", [(i, i ^ 2) for i in range(64)])
    own = total[0] + pair[:NVEC] + near
    theirs = lax.ppermute(own, "grp", [(0, 1), (1, 0)])
    scalars = scalars + lax.ppermute(scalars, "grp", [(0, 1), (1, 0)])
    step_size = scalars[:NVEC] / scalars[NVEC:]
    image = own + theirs + own_noise
    return (step_size[:, None] * targets, targets - step_size[:, None] * image)


def solution(mesh):
    return jax.shard_map(
        on_device,
        mesh=mesh,
        in_specs=(P(None, "blk"), P(None, "blk"), P(), P(), P("blk")),
        out_specs=(P(None, "blk"), P(None, "blk")),
        check_vma=False,
    )
```

```python
import functools
import math

import jax
import jax.numpy as jnp
import numpy as np
from jax import lax
from jax.experimental import pallas as pl
from jax.experimental.pallas import tpu as pltpu
from jax.sharding import PartitionSpec as P

BOTH = ("blk", "grp")
SHARD = 1536
ROWS = 24
CHUNKS = 4
SUPER = SHARD * CHUNKS
NSUPER = 16
NVEC = 16
TALL = 768
WIDE = 512
SUB = 256
UNROLL = 8
LOG2E = math.log2(math.e)
SHIFT = 1.5 * LOG2E
OFFSET = 0.75 * LOG2E * LOG2E
FACTOR = 2.0**SHIFT / (3.0 * LOG2E * LOG2E)
bf16 = jnp.bfloat16
f32 = jnp.float32
f8 = jnp.float8_e5m2


def device_at(block, member):
    return (CHUNKS * block + member // 2) * 2 + member % 2


DISTANCE = [8 - 2 * (m // 2) if m % 2 == 0 else 7 - 2 * ((m // 2) ^ 2) for m in range(8)]


def column_source(a, m):
    s = (a + DISTANCE[m]) % NSUPER
    k, g = m // 2, m % 2
    k ^= 2 * ((a ^ s) & 1)
    even = 8 - 2 * k
    crosses = [s % 8 < even, s % 8 < even - 1]
    return s, k, g ^ (crosses[0] and crosses[1])


def column_route(chunk):
    route = []
    for a in range(NSUPER):
        for m in range(8):
            s, k, g = column_source(a, m)
            route.append((device_at(s, 2 * (k ^ chunk) + g), device_at(a, m)))
    assert len({x for x, _ in route}) == len({x for _, x in route}) == 128
    return route


def row_route(chunk):
    return [
        (device_at(a, ((d // 2) ^ chunk) * 2 + d % 2), device_at(a, d))
        for a in range(NSUPER)
        for d in range(8)
    ]


def backward(route):
    return [(b, a) for a, b in route]


CALLS = [
    ((0, 1, 2, 3), (0,), [(i, 0) for i in range(4)]),
    ((0, 1, 2, 3), (1, 2, 3), [(i, j) for j in (1, 2, 3) for i in range(4)]),
]
OFF = [(1, 0), (2, 1), (3, 1), (0, 2), (0, 3), (2, 3)]
ON = [[(0, 0), (1, 1)], [(2, 2), (3, 3)]]
WITHIN = [(i, j) for j in range(CHUNKS) for i in range(j + 1) if (i, j) not in ((0, 2), (0, 3))]
GIVEN = [(0, 2), (0, 3)]
DOWN, ALONG = SHARD // TALL, SHARD // WIDE


def tile_tables():
    within = [[(i, j, y, x) for i, j in WITHIN for y in range(DOWN) for x in range(ALONG)]] * 2
    tables = []
    for call, (held, columns, pairs) in enumerate(CALLS):

        def tile(i, j, y, x, keep=1):
            return ((held.index(i) * DOWN + y) * TALL, (j * ALONG + x) * WIDE, keep)

        def pair(i, j):
            first = len(held) + columns.index(j)
            return [tile(i, first, y, x) for y in range(DOWN) for x in range(ALONG)]

        regular = [t for i, j in pairs for t in pair(i, j)]
        lists = [regular]
        for half in range(2):
            tiles = [t for i, j in OFF + ON[half] if (i, j) in pairs for t in pair(i, j)]
            fill = len(regular) - len(tiles)
            part, within[half] = within[half][:fill], within[half][fill:]
            lists.append(tiles + [tile(i, held.index(j), y, x, int(i != j)) for i, j, y, x in part])
        given = [(i, j, y, x) for i, j in GIVEN for y in range(DOWN) for x in range(ALONG)]
        for m in range(1, 7):
            k = m // 2
            part = given[2 * m - 2 : 2 * m] if call == 1 else []
            lists.append(regular + [tile(i ^ k, held.index(j ^ k), y, x) for i, j, y, x in part])
        assert all(len(x) % 2 == 0 for x in lists)
        longest = max(len(x) for x in lists)
        tables.append(
            np.array(
                [
                    [v for t in x + x[:1] * (longest - len(x)) for v in t] + [len(x)]
                    for x in lists
                ],
                np.int32,
            )
        )
    assert within == [[], []]
    return tables


def pieces(value, count, dtype=bf16):
    out = []
    for _ in range(count):
        piece = value.astype(dtype).astype(f32)
        out.append(piece)
        value = value - piece
    return out


def kernel_values(squared):
    squared = jnp.maximum(squared, 1e-12)
    shifted = -SHIFT - squared * lax.rsqrt(squared)
    return (shifted * shifted + OFFSET) * jnp.exp2(shifted)


def tile_kernel(x_count, places, begun, *refs):
    refs = list(refs)
    table, scale = refs[:2]
    every = len(places)
    given = 1 + max(array for array, _ in places)
    chunks = [refs[2 + array].at[pl.ds(ROWS * i, ROWS)] for array, i in places]
    rest = refs[2 + given :]
    sums_in, rest = dict(zip(begun, rest)), rest[len(begun) :]
    if begun:
        curve_in, rest = rest[0], rest[1:]
    sums_out, rest = rest[:every], rest[every:]
    curve_out, row_feat, col_feat, vectors, vectors8, row_sum, col_sum, hi0, hi1, lo0, lo1 = rest

    largest = jnp.full((NVEC, 1), 1e-30, f32)
    for chunk in chunks:
        part = jnp.max(jnp.abs(chunk[3:19, :]), axis=1, keepdims=True)
        largest = jnp.maximum(largest, part)
    upward = 1024.0 / largest
    downward = largest * (FACTOR / 1024.0)

    for place, chunk in enumerate(chunks):
        span = slice(place * SHARD, (place + 1) * SHARD)
        scaled = jnp.concatenate(
            [(chunk[c : c + 1, :] - 4.0) * scale[c] for c in range(3)], axis=0
        )
        a1, a2, a3 = pieces(scaled, 3)
        norm = jnp.sum(scaled * scaled, axis=0, keepdims=True)
        n1, n2, n3 = pieces(norm, 3)
        one = jnp.ones_like(norm)
        pad = jnp.zeros((8, SHARD), f32)
        columns = jnp.concatenate(
            [-2.0 * a1, -2.0 * a2, -2.0 * a1, -2.0 * a3, -2.0 * a2, -2.0 * a1,
             one, one, one, n1, n2, n3, pad], axis=0)
        col_feat[:, span] = columns.astype(bf16)
        vec = chunk[3:19, :] * upward
        vectors[:, span] = jnp.concatenate(pieces(vec, 2), axis=0).astype(bf16)
        vectors8[:, span] = jnp.concatenate(pieces(vec, 2, f8), axis=0).astype(f8)
        if place < x_count:
            rows = jnp.concatenate(
                [a1, a1, a2, a1, a2, a3, n1, n2, n3, one, one, one, pad], axis=0
            )
            row_feat[span, :] = jnp.transpose(rows).astype(bf16)
    for ref in (row_sum, col_sum, hi1, lo1):
        ref[...] = jnp.zeros_like(ref)
    count = table[table.shape[0] - 1]

    def place_of(t):
        return (
            pl.multiple_of(table[3 * t], TALL),
            pl.multiple_of(table[3 * t + 1], WIDE),
            table[3 * t + 2],
        )

    def produce(place, hi, lo, x, y):
        row, col, _ = place
        right = col_feat[:, pl.ds(pl.multiple_of(col + x, SUB), SUB)]
        left = row_feat[pl.ds(pl.multiple_of(row + y, SUB), SUB), :]
        value = kernel_values(jnp.dot(left, right, preferred_element_type=f32))
        high = value.astype(bf16)
        hi[y : y + SUB, x : x + SUB] = high
        lo[y : y + SUB, x : x + SUB] = (value - high.astype(f32)).astype(f8)

    def consume_rows(place, part, held, y):
        row, col, _ = place
        across = (((1,), (1,)), ((), ()))
        far = held[:, pl.ds(col, WIDE)]
        row_sum[:, pl.ds(pl.multiple_of(row + y, SUB), SUB)] += lax.dot_general(
            far, part[y : y + SUB, :], across, preferred_element_type=f32
        )

    def consume_columns(place, part, held, x):
        row, col, keep = place
        near = held[:, pl.ds(row, TALL)]
        total = jnp.dot(near, part[:, x : x + SUB], preferred_element_type=f32)
        col_sum[:, pl.ds(pl.multiple_of(col + x, SUB), SUB)] += total * keep.astype(f32)

    def both(ahead, ahead_hi, ahead_lo, now, hi, lo):
        subs = [(x, y) for x in range(0, WIDE, SUB) for y in range(0, TALL, SUB)]
        sides = ((hi, vectors), (lo, vectors8))
        work = [(consume_rows, *side, y) for y in range(0, TALL, SUB) for side in sides]
        work += [(consume_columns, *side, x) for x in range(0, WIDE, SUB) for side in sides]
        done = 0
        for n, (x, y) in enumerate(subs):
            if ahead is not None:
                produce(ahead, ahead_hi, ahead_lo, x, y)
            while done * len(subs) < (n + 1) * len(work) and done < len(work):
                step, part, held, offset = work[done]
                step(now, part, held, offset)
                done += 1

    def two_tiles(t):
        both(place_of(t), hi0, lo0, place_of(jnp.maximum(t - 1, 0)), hi1, lo1)
        both(place_of(t + 1), hi1, lo1, place_of(t), hi0, lo0)

    @pl.loop(0, count // UNROLL)
    def _(u):
        for t in range(0, UNROLL, 2):
            two_tiles(UNROLL * u + t)

    @pl.loop(0, count % UNROLL // 2)
    def _(u):
        two_tiles(count // UNROLL * UNROLL + 2 * u)

    both(None, None, None, place_of(count - 1), hi1, lo1)

    curve = curve_in[...] if begun else jnp.zeros((NVEC, 128), f32)
    for place, chunk in enumerate(chunks):
        span = slice(place * SHARD, (place + 1) * SHARD)
        total = col_sum[:, span]
        if place < x_count:
            total = total + row_sum[:, span]
        total = downward * (total[:NVEC] + total[NVEC:])
        product = total * chunk[3:19, :]
        for lane in range(0, SHARD, 128):
            curve = curve + product[:, lane : lane + 128]
        if place in sums_in:
            total = total + sums_in[place][...]
        sums_out[place][...] = total
    curve_out[...] = curve


def run_tiles(table, scale, rows, columns, sums, curve):
    vmem = pl.BlockSpec(memory_space=pltpu.VMEM)
    smem = pl.BlockSpec(memory_space=pltpu.SMEM)
    count = len(rows) + len(columns)
    wide = len(rows) * SHARD
    every = count * SHARD
    arrays, places = [], []
    for array, i in [*rows, *columns]:
        found = [n for n, other in enumerate(arrays) if other is array]
        if not found:
            arrays.append(array)
        places.append((found[0] if found else len(arrays) - 1, i))
    begun = tuple(i for i, part in enumerate(sums) if part is not None)
    passed = [*arrays, *(sums[i] for i in begun)]
    if begun:
        passed.append(curve)
    out = pl.pallas_call(
        functools.partial(tile_kernel, len(rows), places, begun),
        out_shape=[jax.ShapeDtypeStruct((NVEC, SHARD), f32)] * count
        + [jax.ShapeDtypeStruct((NVEC, 128), f32)],
        in_specs=[smem] * 2 + [vmem] * len(passed),
        out_specs=[vmem] * (count + 1),
        scratch_shapes=[
            pltpu.VMEM((wide, 32), bf16),
            pltpu.VMEM((32, every), bf16),
            pltpu.VMEM((32, every), bf16),
            pltpu.VMEM((32, every), f8),
            pltpu.VMEM((32, wide), f32),
            pltpu.VMEM((32, every), f32),
        ]
        + [pltpu.VMEM((TALL, WIDE), bf16)] * 2
        + [pltpu.VMEM((TALL, WIDE), f8)] * 2,
        compiler_params=pltpu.CompilerParams(vmem_limit_bytes=48 * 2**20),
        cost_estimate=pl.CostEstimate(
            flops=330_000_000 * table.shape[0], bytes_accessed=2_000_000, transcendentals=0
        ),
    )(table, scale, *passed)
    return out[:count], out[count]


def after(value, *others):
    return lax.optimization_barrier((value, *others))[0]


def on_device(points, targets, length_scales, noise_levels, noise_class):
    shard = jnp.concatenate([points, targets, jnp.zeros((ROWS - 19, SHARD), f32)], axis=0)
    swap = [(i, i ^ 1) for i in range(64)]
    first_column = lax.ppermute(shard, BOTH, column_route(0))
    beside = lax.ppermute(shard, "blk", [(i, i ^ 2) for i in range(64)])
    partner = lax.ppermute(shard, "blk", swap)
    across = lax.ppermute(beside, "blk", swap)
    rest = jnp.concatenate([partner, beside, across], axis=0)
    others = lax.ppermute(rest, BOTH, column_route(0))
    rows = {0: (shard, 0), 1: (rest, 0), 2: (rest, 1), 3: (rest, 2)}
    columns = {0: (first_column, 0), 1: (others, 0), 2: (others, 1), 3: (others, 2)}

    block = lax.axis_index("blk")
    member = (block % CHUNKS) * 2 + lax.axis_index("grp")
    variant = jnp.where(member == 0, jnp.where(block < 32, 1, 2), (member + 2) % 9)
    tables = tile_tables()
    scale = (math.sqrt(5.0) * LOG2E) / length_scales

    def sent_back(name):
        kind, c = name
        route = row_route(c) if kind == "x" else column_route(c)
        return lax.ppermute(sums[name], BOTH, backward(route))

    sums, curve = {}, None
    for call, (held, across, _) in enumerate(CALLS):
        names = [("x", c) for c in held] + [("y", c) for c in across]
        parts, curve = run_tiles(
            jnp.asarray(tables[call])[variant], scale, [rows[c] for c in held],
            [columns[c] for c in across], [sums.get(name) for name in names], curve,
        )
        sums.update(zip(names, parts))

    column_sums = jnp.concatenate([sums["y", c] for c in range(CHUNKS)], axis=0)
    column_sums = lax.ppermute(column_sums, BOTH, backward(column_route(0)))

    classes = lax.broadcasted_iota(jnp.int32, (noise_levels.shape[0], noise_class.shape[0]), 0)
    noise_diag = jnp.sum(
        jnp.where(noise_class[None, :] == classes, noise_levels[:, None], 0.0), axis=0
    )
    own_noise = noise_diag[None, :] * targets
    norm = 0.5 * jnp.sum(targets * targets, axis=1)
    curvature = jnp.sum(curve, axis=1) + 0.5 * jnp.sum(targets * own_noise, axis=1)
    scalars = jnp.concatenate([norm, curvature])
    blocks = lax.axis_size("blk")
    scalars = lax.all_to_all(
        jnp.broadcast_to(scalars[None], (blocks, 2 * NVEC)), "blk", 0, 0, tiled=True
    )
    scalars = jnp.sum(scalars, axis=0)

    scalars, column_sums = lax.optimization_barrier((scalars, column_sums))
    total = [sums["x", c] + column_sums[c * NVEC : (c + 1) * NVEC] for c in range(CHUNKS)]
    pair = lax.ppermute(jnp.concatenate([total[1], total[3]], axis=0), "blk", swap)
    near = lax.ppermute(total[2] + pair[NVEC:], "blk", [(i, i ^ 2) for i in range(64)])
    own = total[0] + pair[:NVEC] + near
    theirs = lax.ppermute(own, "grp", [(0, 1), (1, 0)])
    scalars = scalars + lax.ppermute(scalars, "grp", [(0, 1), (1, 0)])
    step_size = scalars[:NVEC] / scalars[NVEC:]
    image = own + theirs + own_noise
    return (step_size[:, None] * targets, targets - step_size[:, None] * image)


def solution(mesh):
    return jax.shard_map(
        on_device,
        mesh=mesh,
        in_specs=(P(None, "blk"), P(None, "blk"), P(), P(), P("blk")),
        out_specs=(P(None, "blk"), P(None, "blk")),
        check_vma=False,
    )
```

```python
import functools
import math

import jax
import jax.numpy as jnp
import numpy as np
from jax import lax
from jax.experimental import pallas as pl
from jax.experimental.pallas import tpu as pltpu
from jax.sharding import PartitionSpec as P

BOTH = ("blk", "grp")
SHARD = 1536
ROWS = 24
DEPTH = 64
CHUNKS = 4
SUPER = SHARD * CHUNKS
NSUPER = 16
NVEC = 16
TALL = 768
WIDE = 512
SUB = 256
UNROLL = 8
LOG2E = math.log2(math.e)
SHIFT = 1.5 * LOG2E
OFFSET = 0.75 * LOG2E * LOG2E
FACTOR = 2.0**SHIFT / (3.0 * LOG2E * LOG2E)
bf16 = jnp.bfloat16
f32 = jnp.float32
f8 = jnp.float8_e5m2


def device_at(block, member):
    return (CHUNKS * block + member // 2) * 2 + member % 2


DISTANCE = [8 - 2 * (m // 2) if m % 2 == 0 else 7 - 2 * ((m // 2) ^ 2) for m in range(8)]


def column_source(a, m):
    s = (a + DISTANCE[m]) % NSUPER
    k, g = m // 2, m % 2
    k ^= 2 * ((a ^ s) & 1)
    even = 8 - 2 * k
    crosses = [s % 8 < even, s % 8 < even - 1]
    return s, k, g ^ (crosses[0] and crosses[1])


def column_route(chunk):
    route = []
    for a in range(NSUPER):
        for m in range(8):
            s, k, g = column_source(a, m)
            route.append((device_at(s, 2 * (k ^ chunk) + g), device_at(a, m)))
    assert len({x for x, _ in route}) == len({x for _, x in route}) == 128
    return route


def row_route(chunk):
    return [
        (device_at(a, ((d // 2) ^ chunk) * 2 + d % 2), device_at(a, d))
        for a in range(NSUPER)
        for d in range(8)
    ]


def backward(route):
    return [(b, a) for a, b in route]


CALLS = [
    ((0, 1, 2, 3), (0,), [(i, 0) for i in range(4)]),
    ((0, 1, 2, 3), (1, 2, 3), [(i, j) for j in (1, 2, 3) for i in range(4)]),
]
OFF = [(1, 0), (2, 1), (3, 1), (0, 2), (0, 3), (2, 3)]
ON = [[(0, 0), (1, 1)], [(2, 2), (3, 3)]]
WITHIN = [(i, j) for j in range(CHUNKS) for i in range(j + 1) if (i, j) not in ((0, 2), (0, 3))]
GIVEN = [(0, 2), (0, 3)]
DOWN, ALONG = SHARD // TALL, SHARD // WIDE


def tile_tables():
    within = [[(i, j, y, x) for i, j in WITHIN for y in range(DOWN) for x in range(ALONG)]] * 2
    tables = []
    for call, (held, columns, pairs) in enumerate(CALLS):

        def tile(i, j, y, x, keep=1):
            return ((held.index(i) * DOWN + y) * TALL, (j * ALONG + x) * WIDE, keep)

        def pair(i, j):
            first = len(held) + columns.index(j)
            return [tile(i, first, y, x) for y in range(DOWN) for x in range(ALONG)]

        regular = [t for i, j in pairs for t in pair(i, j)]
        lists = [regular]
        for half in range(2):
            tiles = [t for i, j in OFF + ON[half] if (i, j) in pairs for t in pair(i, j)]
            fill = len(regular) - len(tiles)
            part, within[half] = within[half][:fill], within[half][fill:]
            lists.append(tiles + [tile(i, held.index(j), y, x, int(i != j)) for i, j, y, x in part])
        given = [(i, j, y, x) for i, j in GIVEN for y in range(DOWN) for x in range(ALONG)]
        for m in range(1, 7):
            k = m // 2
            part = given[2 * m - 2 : 2 * m] if call == 1 else []
            lists.append(regular + [tile(i ^ k, held.index(j ^ k), y, x) for i, j, y, x in part])
        assert all(len(x) % 2 == 0 for x in lists)
        longest = max(len(x) for x in lists)
        tables.append(
            np.array(
                [
                    [v for t in x + x[:1] * (longest - len(x)) for v in t] + [len(x)]
                    for x in lists
                ],
                np.int32,
            )
        )
    assert within == [[], []]
    return tables


def pieces(value, count, dtype=bf16):
    out = []
    for _ in range(count):
        piece = value.astype(dtype).astype(f32)
        out.append(piece)
        value = value - piece
    return out


def kernel_values(squared):
    squared = jnp.maximum(squared, 1e-12)
    shifted = -SHIFT - squared * lax.rsqrt(squared)
    return (shifted * shifted + OFFSET) * jnp.exp2(shifted)


def tile_kernel(x_count, places, begun, *refs):
    refs = list(refs)
    table, scale = refs[:2]
    every = len(places)
    given = 1 + max(array for array, _ in places)
    chunks = [refs[2 + array].at[pl.ds(ROWS * i, ROWS)] for array, i in places]
    rest = refs[2 + given :]
    sums_in, rest = dict(zip(begun, rest)), rest[len(begun) :]
    if begun:
        curve_in, rest = rest[0], rest[1:]
    sums_out, rest = rest[:every], rest[every:]
    curve_out, row_feat, col_feat, vectors, vectors8, row_sum, col_sum, hi0, hi1, lo0, lo1 = rest

    largest = jnp.full((NVEC, 1), 1e-30, f32)
    for chunk in chunks:
        part = jnp.max(jnp.abs(chunk[:NVEC, :]), axis=1, keepdims=True)
        largest = jnp.maximum(largest, part)
    upward = 1024.0 / largest
    downward = largest * (FACTOR / 1024.0)

    line = lax.broadcasted_iota(jnp.int32, (8, SHARD), 0)
    factors = jnp.where(line == 0, scale[0], jnp.where(line == 1, scale[1], scale[2]))

    for place, chunk in enumerate(chunks):
        span = slice(place * SHARD, (place + 1) * SHARD)
        scaled = jnp.where(line < 3, (chunk[NVEC:, :] - 4.0) * factors, 0.0)
        a1, a2, a3 = pieces(scaled, 3)
        norm = jnp.sum(scaled * scaled, axis=0, keepdims=True)
        n1, n2, n3 = pieces(norm, 3)
        norms = jnp.where(line == 0, n1, jnp.where(line == 1, n2, n3))
        pad = jnp.zeros_like(scaled)
        late = jnp.where(line == 3, n1, jnp.where(line == 4, n2, n3))
        tail = jnp.where(line < 3, 1.0, jnp.where(line < 6, late, 0.0))
        columns = jnp.concatenate(
            [-2.0 * a1, -2.0 * a2, -2.0 * a1, -2.0 * a3, -2.0 * a2, -2.0 * a1, tail, pad], axis=0
        )
        col_feat[:, span] = columns.astype(bf16)
        vec = chunk[:NVEC, :] * upward
        vectors[:, span] = jnp.concatenate(pieces(vec, 2), axis=0).astype(bf16)
        vectors8[:, span] = jnp.concatenate(pieces(vec, 2, f8), axis=0).astype(f8)
        if place < x_count:
            tail = jnp.where(line < 3, norms, jnp.where(line < 6, 1.0, 0.0))
            rows = jnp.concatenate([a1, a1, a2, a1, a2, a3, tail, pad], axis=0)
            row_feat[span, :] = jnp.transpose(rows).astype(bf16)
    for ref in (row_sum, col_sum, hi1, lo1):
        ref[...] = jnp.zeros_like(ref)
    count = table[table.shape[0] - 1]

    def place_of(t):
        return (
            pl.multiple_of(table[3 * t], TALL),
            pl.multiple_of(table[3 * t + 1], WIDE),
            table[3 * t + 2],
        )

    def produce(place, hi, lo, x, y):
        row, col, _ = place
        right = col_feat[:, pl.ds(pl.multiple_of(col + x, SUB), SUB)]
        left = row_feat[pl.ds(pl.multiple_of(row + y, SUB), SUB), :]
        value = kernel_values(jnp.dot(left, right, preferred_element_type=f32))
        high = value.astype(bf16)
        hi[y : y + SUB, x : x + SUB] = high
        lo[y : y + SUB, x : x + SUB] = (value - high.astype(f32)).astype(f8)

    def consume_rows(place, part, held, y):
        row, col, _ = place
        across = (((1,), (1,)), ((), ()))
        far = held[:, pl.ds(col, WIDE)]
        row_sum[:, pl.ds(pl.multiple_of(row + y, SUB), SUB)] += lax.dot_general(
            far, part[y : y + SUB, :], across, preferred_element_type=f32
        )

    def consume_columns(place, part, held, x):
        row, col, keep = place
        near = held[:, pl.ds(row, TALL)]
        total = jnp.dot(near, part[:, x : x + SUB], preferred_element_type=f32)
        col_sum[:, pl.ds(pl.multiple_of(col + x, SUB), SUB)] += total * keep.astype(f32)

    def both(ahead, ahead_hi, ahead_lo, now, hi, lo):
        subs = [(x, y) for x in range(0, WIDE, SUB) for y in range(0, TALL, SUB)]
        sides = ((hi, vectors), (lo, vectors8))
        work = [(consume_rows, *side, y) for y in range(0, TALL, SUB) for side in sides]
        work += [(consume_columns, *side, x) for x in range(0, WIDE, SUB) for side in sides]
        done = 0
        for n, (x, y) in enumerate(subs):
            if ahead is not None:
                produce(ahead, ahead_hi, ahead_lo, x, y)
            while done * len(subs) < (n + 1) * len(work) and done < len(work):
                step, part, held, offset = work[done]
                step(now, part, held, offset)
                done += 1

    def two_tiles(t):
        both(place_of(t), hi0, lo0, place_of(jnp.maximum(t - 1, 0)), hi1, lo1)
        both(place_of(t + 1), hi1, lo1, place_of(t), hi0, lo0)

    @pl.loop(0, count // UNROLL)
    def _(u):
        for t in range(0, UNROLL, 2):
            two_tiles(UNROLL * u + t)

    @pl.loop(0, count % UNROLL // 2)
    def _(u):
        two_tiles(count // UNROLL * UNROLL + 2 * u)

    both(None, None, None, place_of(count - 1), hi1, lo1)

    curve = curve_in[...] if begun else jnp.zeros((NVEC, 128), f32)
    for place, chunk in enumerate(chunks):
        span = slice(place * SHARD, (place + 1) * SHARD)
        total = col_sum[:, span]
        if place < x_count:
            total = total + row_sum[:, span]
        total = downward * (total[:NVEC] + total[NVEC:])
        product = total * chunk[:NVEC, :]
        for lane in range(0, SHARD, 128):
            curve = curve + product[:, lane : lane + 128]
        if place in sums_in:
            total = total + sums_in[place][...]
        sums_out[place][...] = total
    curve_out[...] = curve


def run_tiles(table, scale, rows, columns, sums, curve):
    vmem = pl.BlockSpec(memory_space=pltpu.VMEM)
    smem = pl.BlockSpec(memory_space=pltpu.SMEM)
    count = len(rows) + len(columns)
    wide = len(rows) * SHARD
    every = count * SHARD
    arrays, places = [], []
    for array, i in [*rows, *columns]:
        found = [n for n, other in enumerate(arrays) if other is array]
        if not found:
            arrays.append(array)
        places.append((found[0] if found else len(arrays) - 1, i))
    begun = tuple(i for i, part in enumerate(sums) if part is not None)
    passed = [*arrays, *(sums[i] for i in begun)]
    if begun:
        passed.append(curve)
    out = pl.pallas_call(
        functools.partial(tile_kernel, len(rows), places, begun),
        out_shape=[jax.ShapeDtypeStruct((NVEC, SHARD), f32)] * count
        + [jax.ShapeDtypeStruct((NVEC, 128), f32)],
        in_specs=[smem] * 2 + [vmem] * len(passed),
        out_specs=[vmem] * (count + 1),
        scratch_shapes=[
            pltpu.VMEM((wide, DEPTH), bf16),
            pltpu.VMEM((DEPTH, every), bf16),
            pltpu.VMEM((32, every), bf16),
            pltpu.VMEM((32, every), f8),
            pltpu.VMEM((32, wide), f32),
            pltpu.VMEM((32, every), f32),
        ]
        + [pltpu.VMEM((TALL, WIDE), bf16)] * 2
        + [pltpu.VMEM((TALL, WIDE), f8)] * 2,
        compiler_params=pltpu.CompilerParams(vmem_limit_bytes=48 * 2**20),
        cost_estimate=pl.CostEstimate(
            flops=330_000_000 * table.shape[0], bytes_accessed=2_000_000, transcendentals=0
        ),
    )(table, scale, *passed)
    return out[:count], out[count]


def after(value, *others):
    return lax.optimization_barrier((value, *others))[0]


def on_device(points, targets, length_scales, noise_levels, noise_class):
    shard = jnp.concatenate([targets, points, jnp.zeros((ROWS - 19, SHARD), f32)], axis=0)
    swap = [(i, i ^ 1) for i in range(64)]
    first_column = lax.ppermute(shard, BOTH, column_route(0))
    beside = lax.ppermute(shard, "blk", [(i, i ^ 2) for i in range(64)])
    partner = lax.ppermute(shard, "blk", swap)
    across = lax.ppermute(beside, "blk", swap)
    rest = jnp.concatenate([partner, beside, across], axis=0)
    others = lax.ppermute(rest, BOTH, column_route(0))
    rows = {0: (shard, 0), 1: (rest, 0), 2: (rest, 1), 3: (rest, 2)}
    columns = {0: (first_column, 0), 1: (others, 0), 2: (others, 1), 3: (others, 2)}

    block = lax.axis_index("blk")
    member = (block % CHUNKS) * 2 + lax.axis_index("grp")
    variant = jnp.where(member == 0, jnp.where(block < 32, 1, 2), (member + 2) % 9)
    tables = tile_tables()
    scale = (math.sqrt(5.0) * LOG2E) / length_scales

    def sent_back(name):
        kind, c = name
        route = row_route(c) if kind == "x" else column_route(c)
        return lax.ppermute(sums[name], BOTH, backward(route))

    sums, curve = {}, None
    for call, (held, across, _) in enumerate(CALLS):
        names = [("x", c) for c in held] + [("y", c) for c in across]
        parts, curve = run_tiles(
            jnp.asarray(tables[call])[variant], scale, [rows[c] for c in held],
            [columns[c] for c in across], [sums.get(name) for name in names], curve,
        )
        sums.update(zip(names, parts))

    column_sums = jnp.concatenate([sums["y", c] for c in range(CHUNKS)], axis=0)
    column_sums = lax.ppermute(column_sums, BOTH, backward(column_route(0)))

    classes = lax.broadcasted_iota(jnp.int32, (noise_levels.shape[0], noise_class.shape[0]), 0)
    noise_diag = jnp.sum(
        jnp.where(noise_class[None, :] == classes, noise_levels[:, None], 0.0), axis=0
    )
    own_noise = noise_diag[None, :] * targets
    norm = 0.5 * jnp.sum(targets * targets, axis=1)
    curvature = jnp.sum(curve, axis=1) + 0.5 * jnp.sum(targets * own_noise, axis=1)
    scalars = jnp.concatenate([norm, curvature])
    blocks = lax.axis_size("blk")
    scalars = lax.all_to_all(
        jnp.broadcast_to(scalars[None], (blocks, 2 * NVEC)), "blk", 0, 0, tiled=True
    )
    scalars = jnp.sum(scalars, axis=0)

    scalars, column_sums = lax.optimization_barrier((scalars, column_sums))
    total = [sums["x", c] + column_sums[c * NVEC : (c + 1) * NVEC] for c in range(CHUNKS)]
    pair = lax.ppermute(jnp.concatenate([total[1], total[3]], axis=0), "blk", swap)
    near = lax.ppermute(total[2] + pair[NVEC:], "blk", [(i, i ^ 2) for i in range(64)])
    own = total[0] + pair[:NVEC] + near
    theirs = lax.ppermute(own, "grp", [(0, 1), (1, 0)])
    scalars = scalars + lax.ppermute(scalars, "grp", [(0, 1), (1, 0)])
    step_size = scalars[:NVEC] / scalars[NVEC:]
    image = own + theirs + own_noise
    return (step_size[:, None] * targets, targets - step_size[:, None] * image)


def solution(mesh):
    return jax.shard_map(
        on_device,
        mesh=mesh,
        in_specs=(P(None, "blk"), P(None, "blk"), P(), P(), P("blk")),
        out_specs=(P(None, "blk"), P(None, "blk")),
        check_vma=False,
    )
```

```python
import functools
import math

import jax
import jax.numpy as jnp
import numpy as np
from jax import lax
from jax.experimental import pallas as pl
from jax.experimental.pallas import tpu as pltpu
from jax.sharding import PartitionSpec as P

BOTH = ("blk", "grp")
SHARD = 1536
ROWS = 24
DEPTH = 64
CHUNKS = 4
SUPER = SHARD * CHUNKS
NSUPER = 16
NVEC = 16
TALL = 768
WIDE = 512
SUB = 256
UNROLL = 12
LOG2E = math.log2(math.e)
SHIFT = 1.5 * LOG2E
OFFSET = 0.75 * LOG2E * LOG2E
FACTOR = 2.0**SHIFT / (3.0 * LOG2E * LOG2E)
bf16 = jnp.bfloat16
f32 = jnp.float32
f8 = jnp.float8_e5m2


def device_at(block, member):
    return (CHUNKS * block + member // 2) * 2 + member % 2


DISTANCE = [8 - 2 * (m // 2) if m % 2 == 0 else 7 - 2 * ((m // 2) ^ 2) for m in range(8)]


def column_source(a, m):
    s = (a + DISTANCE[m]) % NSUPER
    k, g = m // 2, m % 2
    k ^= 2 * ((a ^ s) & 1)
    even = 8 - 2 * k
    crosses = [s % 8 < even, s % 8 < even - 1]
    return s, k, g ^ (crosses[0] and crosses[1])


def column_route(chunk):
    route = []
    for a in range(NSUPER):
        for m in range(8):
            s, k, g = column_source(a, m)
            route.append((device_at(s, 2 * (k ^ chunk) + g), device_at(a, m)))
    assert len({x for x, _ in route}) == len({x for _, x in route}) == 128
    return route


def row_route(chunk):
    return [
        (device_at(a, ((d // 2) ^ chunk) * 2 + d % 2), device_at(a, d))
        for a in range(NSUPER)
        for d in range(8)
    ]


def backward(route):
    return [(b, a) for a, b in route]


CALLS = [
    ((0, 1, 2, 3), (0,), [(i, 0) for i in range(4)]),
    ((0, 1, 2, 3), (1, 2, 3), [(i, j) for j in (1, 2, 3) for i in range(4)]),
]
OFF = [(1, 0), (2, 1), (3, 1), (0, 2), (0, 3), (2, 3)]
ON = [[(0, 0), (1, 1)], [(2, 2), (3, 3)]]
WITHIN = [(i, j) for j in range(CHUNKS) for i in range(j + 1) if (i, j) not in ((0, 2), (0, 3))]
GIVEN = [(0, 2), (0, 3)]
DOWN, ALONG = SHARD // TALL, SHARD // WIDE


def tile_tables():
    within = [[(i, j, y, x) for i, j in WITHIN for y in range(DOWN) for x in range(ALONG)]] * 2
    tables = []
    for call, (held, columns, pairs) in enumerate(CALLS):

        def tile(i, j, y, x, keep=1):
            return ((held.index(i) * DOWN + y) * TALL, (j * ALONG + x) * WIDE, keep)

        def pair(i, j):
            first = len(held) + columns.index(j)
            return [tile(i, first, y, x) for y in range(DOWN) for x in range(ALONG)]

        regular = [t for i, j in pairs for t in pair(i, j)]
        lists = [regular]
        for half in range(2):
            tiles = [t for i, j in OFF + ON[half] if (i, j) in pairs for t in pair(i, j)]
            fill = len(regular) - len(tiles)
            part, within[half] = within[half][:fill], within[half][fill:]
            lists.append(tiles + [tile(i, held.index(j), y, x, int(i != j)) for i, j, y, x in part])
        given = [(i, j, y, x) for i, j in GIVEN for y in range(DOWN) for x in range(ALONG)]
        for m in range(1, 7):
            k = m // 2
            part = given[2 * m - 2 : 2 * m] if call == 1 else []
            lists.append(regular + [tile(i ^ k, held.index(j ^ k), y, x) for i, j, y, x in part])
        assert all(len(x) % 2 == 0 for x in lists)
        longest = max(len(x) for x in lists)
        tables.append(
            np.array(
                [
                    [v for t in x + x[:1] * (longest - len(x)) for v in t] + [len(x)]
                    for x in lists
                ],
                np.int32,
            )
        )
    assert within == [[], []]
    return tables


def pieces(value, count, dtype=bf16):
    out = []
    for _ in range(count):
        piece = value.astype(dtype).astype(f32)
        out.append(piece)
        value = value - piece
    return out


def kernel_values(squared):
    squared = jnp.maximum(squared, 1e-12)
    shifted = -SHIFT - squared * lax.rsqrt(squared)
    return (shifted * shifted + OFFSET) * jnp.exp2(shifted)


def tile_kernel(x_count, places, begun, *refs):
    refs = list(refs)
    table, scale = refs[:2]
    every = len(places)
    given = 1 + max(array for array, _ in places)
    chunks = [refs[2 + array].at[pl.ds(ROWS * i, ROWS)] for array, i in places]
    rest = refs[2 + given :]
    sums_in, rest = dict(zip(begun, rest)), rest[len(begun) :]
    if begun:
        curve_in, rest = rest[0], rest[1:]
    sums_out, rest = rest[:every], rest[every:]
    curve_out, row_feat, col_feat, vectors, vectors8, row_sum, col_sum, hi0, hi1, lo0, lo1 = rest

    largest = jnp.full((NVEC, 1), 1e-30, f32)
    for chunk in chunks:
        part = jnp.max(jnp.abs(chunk[:NVEC, :]), axis=1, keepdims=True)
        largest = jnp.maximum(largest, part)
    upward = 1024.0 / largest
    downward = largest * (FACTOR / 1024.0)

    line = lax.broadcasted_iota(jnp.int32, (8, SHARD), 0)
    factors = jnp.where(line == 0, scale[0], jnp.where(line == 1, scale[1], scale[2]))

    for place, chunk in enumerate(chunks):
        span = slice(place * SHARD, (place + 1) * SHARD)
        scaled = jnp.where(line < 3, (chunk[NVEC:, :] - 4.0) * factors, 0.0)
        a1, a2, a3 = pieces(scaled, 3)
        norm = jnp.sum(scaled * scaled, axis=0, keepdims=True)
        n1, n2, n3 = pieces(norm, 3)
        norms = jnp.where(line == 0, n1, jnp.where(line == 1, n2, n3))
        pad = jnp.zeros_like(scaled)
        late = jnp.where(line == 3, n1, jnp.where(line == 4, n2, n3))
        tail = jnp.where(line < 3, 1.0, jnp.where(line < 6, late, 0.0))
        columns = jnp.concatenate(
            [-2.0 * a1, -2.0 * a2, -2.0 * a1, -2.0 * a3, -2.0 * a2, -2.0 * a1, tail, pad], axis=0
        )
        col_feat[:, span] = columns.astype(bf16)
        vec = chunk[:NVEC, :] * upward
        vectors[:, span] = jnp.concatenate(pieces(vec, 2), axis=0).astype(bf16)
        vectors8[:, span] = jnp.concatenate(pieces(vec, 2, f8), axis=0).astype(f8)
        if place < x_count:
            tail = jnp.where(line < 3, norms, jnp.where(line < 6, 1.0, 0.0))
            rows = jnp.concatenate([a1, a1, a2, a1, a2, a3, tail, pad], axis=0)
            row_feat[span, :] = jnp.transpose(rows).astype(bf16)
    for ref in (row_sum, col_sum, hi1, lo1):
        ref[...] = jnp.zeros_like(ref)
    count = table[table.shape[0] - 1]

    def place_of(t):
        return (
            pl.multiple_of(table[3 * t], TALL),
            pl.multiple_of(table[3 * t + 1], WIDE),
            table[3 * t + 2],
        )

    def produce(place, hi, lo, x, y):
        row, col, _ = place
        right = col_feat[:, pl.ds(pl.multiple_of(col + x, SUB), SUB)]
        left = row_feat[pl.ds(pl.multiple_of(row + y, SUB), SUB), :]
        value = kernel_values(jnp.dot(left, right, preferred_element_type=f32))
        high = value.astype(bf16)
        hi[y : y + SUB, x : x + SUB] = high
        lo[y : y + SUB, x : x + SUB] = (value - high.astype(f32)).astype(f8)

    def consume_rows(place, part, held, y):
        row, col, _ = place
        across = (((1,), (1,)), ((), ()))
        far = held[:, pl.ds(col, WIDE)]
        row_sum[:, pl.ds(pl.multiple_of(row + y, SUB), SUB)] += lax.dot_general(
            far, part[y : y + SUB, :], across, preferred_element_type=f32
        )

    def consume_columns(place, part, held, x):
        row, col, keep = place
        near = held[:, pl.ds(row, TALL)]
        total = jnp.dot(near, part[:, x : x + SUB], preferred_element_type=f32)
        col_sum[:, pl.ds(pl.multiple_of(col + x, SUB), SUB)] += total * keep.astype(f32)

    def both(ahead, ahead_hi, ahead_lo, now, hi, lo):
        subs = [(x, y) for x in range(0, WIDE, SUB) for y in range(0, TALL, SUB)]
        sides = ((hi, vectors), (lo, vectors8))
        work = [(consume_rows, *side, y) for side in sides for y in range(0, TALL, SUB)]
        work += [(consume_columns, *side, x) for side in sides for x in range(0, WIDE, SUB)]
        done = 0
        for n, (x, y) in enumerate(subs):
            if ahead is not None:
                produce(ahead, ahead_hi, ahead_lo, x, y)
            while done * len(subs) < (n + 1) * len(work) and done < len(work):
                step, part, held, offset = work[done]
                step(now, part, held, offset)
                done += 1

    def two_tiles(t):
        both(place_of(t), hi0, lo0, place_of(jnp.maximum(t - 1, 0)), hi1, lo1)
        both(place_of(t + 1), hi1, lo1, place_of(t), hi0, lo0)

    @pl.loop(0, count // UNROLL)
    def _(u):
        for t in range(0, UNROLL, 2):
            two_tiles(UNROLL * u + t)

    @pl.loop(0, count % UNROLL // 2)
    def _(u):
        two_tiles(count // UNROLL * UNROLL + 2 * u)

    both(None, None, None, place_of(count - 1), hi1, lo1)

    curve = curve_in[...] if begun else jnp.zeros((NVEC, 128), f32)
    for place, chunk in enumerate(chunks):
        span = slice(place * SHARD, (place + 1) * SHARD)
        total = col_sum[:, span]
        if place < x_count:
            total = total + row_sum[:, span]
        total = downward * (total[:NVEC] + total[NVEC:])
        product = total * chunk[:NVEC, :]
        for lane in range(0, SHARD, 128):
            curve = curve + product[:, lane : lane + 128]
        if place in sums_in:
            total = total + sums_in[place][...]
        sums_out[place][...] = total
    curve_out[...] = curve


def run_tiles(table, scale, rows, columns, sums, curve):
    vmem = pl.BlockSpec(memory_space=pltpu.VMEM)
    smem = pl.BlockSpec(memory_space=pltpu.SMEM)
    count = len(rows) + len(columns)
    wide = len(rows) * SHARD
    every = count * SHARD
    arrays, places = [], []
    for array, i in [*rows, *columns]:
        found = [n for n, other in enumerate(arrays) if other is array]
        if not found:
            arrays.append(array)
        places.append((found[0] if found else len(arrays) - 1, i))
    begun = tuple(i for i, part in enumerate(sums) if part is not None)
    passed = [*arrays, *(sums[i] for i in begun)]
    if begun:
        passed.append(curve)
    out = pl.pallas_call(
        functools.partial(tile_kernel, len(rows), places, begun),
        out_shape=[jax.ShapeDtypeStruct((NVEC, SHARD), f32)] * count
        + [jax.ShapeDtypeStruct((NVEC, 128), f32)],
        in_specs=[smem] * 2 + [vmem] * len(passed),
        out_specs=[vmem] * (count + 1),
        scratch_shapes=[
            pltpu.VMEM((wide, DEPTH), bf16),
            pltpu.VMEM((DEPTH, every), bf16),
            pltpu.VMEM((32, every), bf16),
            pltpu.VMEM((32, every), f8),
            pltpu.VMEM((32, wide), f32),
            pltpu.VMEM((32, every), f32),
        ]
        + [pltpu.VMEM((TALL, WIDE), bf16)] * 2
        + [pltpu.VMEM((TALL, WIDE), f8)] * 2,
        compiler_params=pltpu.CompilerParams(vmem_limit_bytes=48 * 2**20),
        cost_estimate=pl.CostEstimate(
            flops=330_000_000 * table.shape[0], bytes_accessed=2_000_000, transcendentals=0
        ),
    )(table, scale, *passed)
    return out[:count], out[count]


def after(value, *others):
    return lax.optimization_barrier((value, *others))[0]


def on_device(points, targets, length_scales, noise_levels, noise_class):
    shard = jnp.concatenate([targets, points, jnp.zeros((ROWS - 19, SHARD), f32)], axis=0)
    swap = [(i, i ^ 1) for i in range(64)]
    first_column = lax.ppermute(shard, BOTH, column_route(0))
    beside = lax.ppermute(shard, "blk", [(i, i ^ 2) for i in range(64)])
    partner = lax.ppermute(shard, "blk", swap)
    across = lax.ppermute(beside, "blk", swap)
    rest = jnp.concatenate([partner, beside, across], axis=0)
    others = lax.ppermute(rest, BOTH, column_route(0))
    rows = {0: (shard, 0), 1: (rest, 0), 2: (rest, 1), 3: (rest, 2)}
    columns = {0: (first_column, 0), 1: (others, 0), 2: (others, 1), 3: (others, 2)}

    block = lax.axis_index("blk")
    member = (block % CHUNKS) * 2 + lax.axis_index("grp")
    variant = jnp.where(member == 0, jnp.where(block < 32, 1, 2), (member + 2) % 9)
    tables = tile_tables()
    scale = (math.sqrt(5.0) * LOG2E) / length_scales

    def sent_back(name):
        kind, c = name
        route = row_route(c) if kind == "x" else column_route(c)
        return lax.ppermute(sums[name], BOTH, backward(route))

    sums, curve = {}, None
    for call, (held, across, _) in enumerate(CALLS):
        names = [("x", c) for c in held] + [("y", c) for c in across]
        parts, curve = run_tiles(
            jnp.asarray(tables[call])[variant], scale, [rows[c] for c in held],
            [columns[c] for c in across], [sums.get(name) for name in names], curve,
        )
        sums.update(zip(names, parts))

    column_sums = jnp.concatenate([sums["y", c] for c in range(CHUNKS)], axis=0)
    column_sums = lax.ppermute(column_sums, BOTH, backward(column_route(0)))

    classes = lax.broadcasted_iota(jnp.int32, (noise_levels.shape[0], noise_class.shape[0]), 0)
    noise_diag = jnp.sum(
        jnp.where(noise_class[None, :] == classes, noise_levels[:, None], 0.0), axis=0
    )
    own_noise = noise_diag[None, :] * targets
    norm = 0.5 * jnp.sum(targets * targets, axis=1)
    curvature = jnp.sum(curve, axis=1) + 0.5 * jnp.sum(targets * own_noise, axis=1)
    scalars = jnp.concatenate([norm, curvature])
    blocks = lax.axis_size("blk")
    scalars = lax.all_to_all(
        jnp.broadcast_to(scalars[None], (blocks, 2 * NVEC)), "blk", 0, 0, tiled=True
    )
    scalars = jnp.sum(scalars, axis=0)

    scalars, column_sums = lax.optimization_barrier((scalars, column_sums))
    total = [sums["x", c] + column_sums[c * NVEC : (c + 1) * NVEC] for c in range(CHUNKS)]
    pair = lax.ppermute(jnp.concatenate([total[1], total[3]], axis=0), "blk", swap)
    near = lax.ppermute(total[2] + pair[NVEC:], "blk", [(i, i ^ 2) for i in range(64)])
    own = total[0] + pair[:NVEC] + near
    theirs = lax.ppermute(own, "grp", [(0, 1), (1, 0)])
    scalars = scalars + lax.ppermute(scalars, "grp", [(0, 1), (1, 0)])
    step_size = scalars[:NVEC] / scalars[NVEC:]
    image = own + theirs + own_noise
    return (step_size[:, None] * targets, targets - step_size[:, None] * image)


def solution(mesh):
    return jax.shard_map(
        on_device,
        mesh=mesh,
        in_specs=(P(None, "blk"), P(None, "blk"), P(), P(), P("blk")),
        out_specs=(P(None, "blk"), P(None, "blk")),
        check_vma=False,
    )
```
